256 devices in a mesh: row: 32 (over y_hi, z, core), col: 8 (over x, y_lo).
Axes of the slice: x: 4, y: 4 (y_hi: 2, y_lo: 2; y = y_hi * 2 + y_lo), z: 8, core: 2. Of those that a mesh axis runs over, the one named last changes fastest.
Arguments:
- queries: bfloat16 [3072, 7168], P('row', 'col'), may hold values from -8 to 8
- key_rows: bfloat16 [3072, 7168], P('row', 'col'), may hold values from -8 to 8
- value_rows: bfloat16 [3072, 7168], P('row', 'col'), may hold values from -6 to 6
- saved_output: bfloat16 [3072, 7168], P('row', 'col'), may hold values from -4 to 4
- grad_output: bfloat16 [3072, 7168], P('row', 'col'), may hold values from -6 to 6
- pair_bias: bfloat16 [2, 3072, 3072], P(None, 'row', 'col'), may hold values from -6 to 6
- chain_id: int32 [3072], replicated, may hold values from 0 to 7, as said below
- allowed_pairs: int32 [8, 8], replicated, may hold values from 0 to 1, as said below
Outputs:
- grad_queries: bfloat16 [3072, 7168], P('row', 'col')
- grad_keys: bfloat16 [3072, 7168], P('row', 'col')
- grad_values: bfloat16 [3072, 7168], P('row', 'col')
- grad_bias: bfloat16 [2, 3072, 3072], P(None, 'row', 'col')
The draws below stay inside these ranges and needn't reach their ends.
Inputs may be any that keep to these rules, and one draw needn't show every extreme that they name: `chain_id`: chain numbers never fall along the tokens and each of the 8 chains holds at least one token. `allowed_pairs`: symmetric, with ones on the diagonal.
All inputs are finite; a program needn't handle non-finite values.
Results may differ from the reference program's by a relative error of at most 0.022.
Values may be sent and summed in bfloat16 or wider, within the bound.
No kernel may reach another device: no remote copies, remote signals or barrier semaphores. Data moves between devices by JAX's collectives and lax.ppermute only.
A program may use at most 128 MiB of HBM per device.

```python
import math
import jax
import jax.numpy as jnp
from jax import lax

H = 2
DH = 32
CHAINS = 8
TOKENS = 3072
COLS = 112
N_ROW = 32


def chain_cuts(key):
    order = jax.random.permutation(key, TOKENS - 1)
    cuts = order[:CHAINS - 1].astype(jnp.int32) + 1
    positions = jnp.arange(TOKENS, dtype=jnp.int32)
    return jnp.sum((positions[:, None] >= cuts[None, :]).astype(jnp.int32), axis=1).astype(jnp.int32)


def draw_chain_id(key, part):
    chain = chain_cuts(key)
    return chain


def draw_allowed_pairs(key, part):
    key = jax.random.fold_in(key, 2)
    coins = jax.random.randint(key, (CHAINS, CHAINS), 0, 2, dtype=jnp.int32)
    upper = jnp.triu(coins, 1)
    table = upper + upper.T + jnp.eye(CHAINS, dtype=jnp.int32)
    table = table.at[0, CHAINS - 1].set(0)
    table = table.at[CHAINS - 1, 0].set(0)
    return table.astype(jnp.int32)


def draw_queries(key, part):
    key = jax.random.fold_in(key, 3)
    shape = (TOKENS, COLS * H * DH)
    return jnp.clip(jax.random.normal(key, shape, jnp.float32), -8.0, 8.0).astype(jnp.bfloat16)


def draw_key_rows(key, part):
    key = jax.random.fold_in(key, 4)
    shape = (TOKENS, COLS * H * DH)
    return jnp.clip(jax.random.normal(key, shape, jnp.float32), -8.0, 8.0).astype(jnp.bfloat16)


def shard_levels(rng, dims, split, least, largest):
    def one(position, parts):
        steps = jax.random.uniform(jax.random.fold_in(jax.random.fold_in(rng, 6), position), (parts,), jnp.float32, least / len(split), largest / len(split))
        return jnp.repeat(jnp.exp(steps), dims[position] // parts).reshape((-1,) + (1,) * (len(dims) - position - 1))

    level = one(*split[0])
    for cut in split[1:]:
        level = level * one(*cut)
    return level


def scatter_about(stream_key, shape, spread, reach, cuts=(), kind=jnp.bfloat16):
    drawn = jax.random.normal(stream_key, shape, jnp.float32) * spread
    if len(cuts) > 0:
        drawn = shard_levels(stream_key, shape, cuts, -0.22, 0.18) * drawn
    return jnp.clip(drawn, min=-reach, max=reach).astype(kind)


def setup_inputs(seed: int = 0) -> dict:
    arg_keys = jax.random.split(jax.random.key(seed), 9)
    return {
        "queries": draw_queries(jax.random.fold_in(arg_keys[8], 71), 0),
        "key_rows": draw_key_rows(jax.random.fold_in(arg_keys[8], 71), 0),
        "value_rows": scatter_about(arg_keys[2], (TOKENS, COLS * H * DH), 1.0, 6.0, ((0, 32), (1, 8))),
        "saved_output": scatter_about(arg_keys[3], (TOKENS, COLS * H * DH), 0.5, 4.0, ((0, 32), (1, 8))),
        "grad_output": scatter_about(arg_keys[4], (TOKENS, COLS * H * DH), 1.0, 6.0, ((0, 32), (1, 8))),
        "pair_bias": scatter_about(arg_keys[5], (H, TOKENS, TOKENS), 1.0, 6.0, ((1, 32), (2, 8))),
        "chain_id": draw_chain_id(jax.random.fold_in(arg_keys[8], 71), 0),
        "allowed_pairs": draw_allowed_pairs(jax.random.fold_in(arg_keys[8], 71), 0),
    }


MASKED = -1000000000.0

def round_half(value):
    return lax.optimization_barrier(value.astype(jnp.bfloat16)).astype(jnp.float32)

def reference(queries, key_rows, value_rows, saved_output, grad_output, pair_bias, chain_id, allowed_pairs):
    token_count = queries.shape[0]
    head_width = H * DH
    col_count = queries.shape[1] // head_width
    slab_rows = token_count // N_ROW
    score_scale = 1.0 / math.sqrt(DH)
    active = allowed_pairs[chain_id[:, None], chain_id[None, :]] == 1
    bias_full = pair_bias.astype(jnp.float32)

    def to_columns(array):
        return array.reshape(token_count, col_count, H, DH).transpose(1, 0, 2, 3).astype(jnp.float32)
    column_items = (to_columns(queries), to_columns(key_rows), to_columns(value_rows), to_columns(saved_output), to_columns(grad_output))

    def column(bias_sum, column_data):
        q_col, k_col, v_col, o_col, g_col = column_data
        logits = jnp.einsum('ihd,khd->hik', q_col, k_col) * score_scale + bias_full
        logits = jnp.where(active[None], logits, MASKED)
        row_max = lax.optimization_barrier(jnp.max(logits, axis=2, keepdims=True))
        exponent = jnp.exp(logits - row_max)
        weights = exponent / lax.optimization_barrier(jnp.sum(exponent, axis=2, keepdims=True))
        row_delta = lax.optimization_barrier(jnp.sum(g_col * o_col, axis=2)).T
        dweights = jnp.einsum('ihd,khd->hik', g_col, v_col)
        dlogits = weights * (dweights - row_delta[:, :, None])
        weights_half = round_half(weights)
        dlogits_half = round_half(dlogits)
        grad_q = jnp.einsum('hik,khd->ihd', dlogits_half, k_col) * score_scale
        q_slabs = q_col.reshape(N_ROW, slab_rows, H, DH)
        g_slabs = g_col.reshape(N_ROW, slab_rows, H, DH)
        dl_slabs = dlogits_half.reshape(H, N_ROW, slab_rows, token_count)
        w_slabs = weights_half.reshape(H, N_ROW, slab_rows, token_count)
        key_parts = jnp.einsum('hrik,rihd->rkhd', dl_slabs, q_slabs) * score_scale
        value_parts = jnp.einsum('hrik,rihd->rkhd', w_slabs, g_slabs)
        grad_k = lax.optimization_barrier(jnp.sum(round_half(key_parts), axis=0))
        grad_v = lax.optimization_barrier(jnp.sum(round_half(value_parts), axis=0))
        return (bias_sum + dlogits, (grad_q, grad_k, grad_v))
    bias_start = jnp.zeros((H, token_count, token_count), jnp.float32)
    bias_sum, (grad_q, grad_k, grad_v) = lax.scan(column, bias_start, column_items)

    def to_rows(array):
        return array.transpose(1, 0, 2, 3).reshape(token_count, col_count * head_width).astype(jnp.bfloat16)
    return (to_rows(grad_q), to_rows(grad_k), to_rows(grad_v), bias_sum.astype(jnp.bfloat16))
```

```python
import functools
import math

import jax
import jax.numpy as jnp
from jax import lax
from jax.experimental import pallas as pl
from jax.experimental.pallas import tpu as pltpu
from jax.sharding import PartitionSpec as P

H = 2
DH = 32
SCALE = 1.0 / math.sqrt(DH)
LOG2E = math.log2(math.e)
MASKED = -1000000000.0 * LOG2E
NY, NZ, NC = 2, 8, 2
NX, NL = 4, 2
HALF = 7
CHUNKS = (4, 3)
KT = 1024

F32 = jnp.float32
BF = jnp.bfloat16
NT = (((1,), (1,)), ((), ()))
VMEM = pl.BlockSpec(memory_space=pltpu.VMEM)
SMEM = pl.BlockSpec(memory_space=pltpu.SMEM)
PARAMS = pltpu.CompilerParams(vmem_limit_bytes=56 * 2**20)


def iota(shape, dim):
    return lax.broadcasted_iota(jnp.int32, shape, dim)


def row_move(array, dy, dz, dc):
    pairs = []
    for y in range(NY):
        for z in range(NZ):
            for c in range(NC):
                target = ((y ^ dy) * NZ + (z + dz) % NZ) * NC + (c ^ dc)
                pairs.append(((y * NZ + z) * NC + c, target))
    return lax.ppermute(array, "row", pairs)


def col_move(array, dx, dl):
    pairs = []
    for x in range(NX):
        for l in range(NL):
            pairs.append((x * NL + l, ((x + dx) % NX) * NL + (l ^ dl)))
    return lax.ppermute(array, "col", pairs)


def place(owner, first, width, shape, dim):
    index = iota(shape, dim)
    head, half = owner // 2, owner % 2
    return (half * HALF + first + index // DH) * (H * DH) + head * DH + index % DH


def split_kernel(rows, width, me_ref, q_ref, k_ref, v_ref, o_ref, g_ref, *outs):
    for f in range(4):
        owner = me_ref[0] ^ f
        first = 0
        for n, cols in enumerate(CHUNKS):
            w = cols * DH
            pick = (
                iota((width, w), 0) == place(owner, first, w, (width, w), 1)
            ).astype(BF)
            kv_out, qgo_out = outs[2 * (f * len(CHUNKS) + n)], outs[2 * (f * len(CHUNKS) + n) + 1]
            for u, ref in enumerate((k_ref, v_ref)):
                kv_out[:, u * w : (u + 1) * w] = jnp.dot(
                    ref[...], pick, preferred_element_type=F32
                ).astype(BF)
            for u, ref in enumerate((q_ref, g_ref, o_ref)):
                qgo_out[:, u * w : (u + 1) * w] = jnp.dot(
                    ref[...], pick, preferred_element_type=F32
                ).astype(BF)
            first += cols


def split(me, arrays):
    rows, width = arrays[0].shape
    shapes = []
    for f in range(4):
        for cols in CHUNKS:
            shapes.append(jax.ShapeDtypeStruct((rows, 2 * cols * DH), BF))
            shapes.append(jax.ShapeDtypeStruct((rows, 3 * cols * DH), BF))
    return pl.pallas_call(
        functools.partial(split_kernel, rows, width),
        in_specs=[SMEM] + [VMEM] * 5,
        out_specs=[VMEM] * len(shapes),
        out_shape=shapes,
        compiler_params=PARAMS,
        name="split",
    )(me, *arrays)


def join_kernel(rows, width, me_ref, *refs):
    n = 4 * len(CHUNKS)
    dq, dkv, outs = refs[:n], refs[n : 2 * n], refs[2 * n :]
    sums = [jnp.zeros((rows, width), F32)] * 3
    for f in range(4):
        owner = me_ref[0] ^ f
        first = 0
        for m, cols in enumerate(CHUNKS):
            w = cols * DH
            spread = (
                iota((w, width), 1) == place(owner, first, w, (w, width), 0)
            ).astype(BF)
            a, b = dq[f * len(CHUNKS) + m], dkv[f * len(CHUNKS) + m]
            parts = (a[...], b[:, :w], b[:, w:])
            for u in range(3):
                sums[u] = sums[u] + jnp.dot(parts[u], spread, preferred_element_type=F32)
            first += cols
    for u in range(3):
        outs[u][...] = sums[u].astype(BF)


def join(me, rows, width, dq, dkv):
    return pl.pallas_call(
        functools.partial(join_kernel, rows, width),
        in_specs=[SMEM] + [VMEM] * (len(dq) + len(dkv)),
        out_specs=[VMEM] * 3,
        out_shape=[jax.ShapeDtypeStruct((rows, width), BF)] * 3,
        compiler_params=PARAMS,
        name="join",
    )(me, *dq, *dkv)


def bias_kernel(rows, keys, pos_ref, reach_ref, chain_ref, *refs):
    pieces, out_ref = refs[:8], refs[8]
    x, l = pos_ref[3], pos_ref[4]
    for xs in range(NX):
        for fl in range(NL):
            block = ((x + xs) % NX) * NL + (l ^ fl)
            lanes = pl.ds(pl.multiple_of(block * keys, keys), keys)
            hot = (chain_ref[:, lanes] == iota((8, keys), 0)).astype(BF)
            for fy in range(2):
                for fc in range(2):
                    f = fy * 2 + fc
                    part = pieces[fc * NX + xs][fl, fy].astype(F32)
                    reach = jnp.dot(
                        reach_ref[f * rows : (f + 1) * rows, :], hot, preferred_element_type=F32
                    )
                    out_ref[f * rows : (f + 1) * rows, lanes] = jnp.where(
                        reach > 0.5, part * LOG2E, MASKED
                    )


def attn_kernel(rows, keys, cols, first, last, pos_ref, *refs):
    tokens = 32 * rows
    R = 4 * rows
    w = cols * DH
    qgo_refs, kv_refs, b2_ref = refs[0:4], refs[4:12], refs[12]
    refs = refs[13:]
    if not first:
        db_in, refs = refs[0], refs[1:]
    dq_out, dkv_out = refs[0:2]
    if last:
        own_out, other_out = refs[2:4]
        refs = refs[4:]
    else:
        db_out = refs[2]
        refs = refs[3:]
    kn, kvt, qcat, gcat, qt, gt, t_ref, acc, dq_acc = refs[:9]
    db_ref = refs[9] if last else db_out
    me, z = pos_ref[0], pos_ref[2]
    my, mc = me // 2, me % 2
    wide = acc.shape[0]

    def natural(s, f):
        return ((my ^ (f // 2)) * NZ + (z + s) % NZ) * NC + (mc ^ (f % 2))

    for s in range(NZ):
        for f in range(4):
            kn[natural(s, f)] = kv_refs[s][f]
    eye = (iota((2 * w, 2 * w), 0) == iota((2 * w, 2 * w), 1)).astype(BF)
    for n in range(4):
        part = kn[n * 8 : (n + 1) * 8].reshape(8 * rows, 2 * w)
        kvt[:, n * 8 * rows : (n + 1) * 8 * rows] = lax.dot_general(
            eye, part, NT, preferred_element_type=F32
        ).astype(BF)
    eye_w = (iota((w, w), 0) == iota((w, w), 1)).astype(BF)
    q = jnp.concatenate([qgo_refs[f][:, :w] for f in range(4)], axis=0)
    g = jnp.concatenate([qgo_refs[f][:, w : 2 * w] for f in range(4)], axis=0)
    o = jnp.concatenate([qgo_refs[f][:, 2 * w :] for f in range(4)], axis=0)
    qt[...] = lax.dot_general(eye_w, q, NT, preferred_element_type=F32).astype(BF)
    gt[...] = lax.dot_general(eye_w, g, NT, preferred_element_type=F32).astype(BF)
    qs = q.astype(F32) * (SCALE * LOG2E)
    q_hi = qs.astype(BF)
    q_lo = (qs - q_hi.astype(F32)).astype(BF)
    go = g.astype(F32) * o.astype(F32)
    go_hi = go.astype(BF)
    go_lo = (go - go_hi.astype(F32)).astype(BF)
    for c in range(cols):
        at = slice(c * DH, (c + 1) * DH)
        qcat[c] = jnp.concatenate([q_hi[:, at], q_lo[:, at]], axis=1)
        gcat[c] = jnp.concatenate([g[:, at], go_hi[:, at], go_lo[:, at]], axis=1)
    if first:
        db_ref[...] = jnp.zeros_like(db_ref)
    else:
        db_ref[...] = db_in[...]
    dq_acc[...] = jnp.zeros_like(dq_acc)
    minus = jnp.full((2 * DH, KT), -1.0, BF)
    tiles = tokens // KT

    def column(c, _):
        k_at = pl.ds(pl.multiple_of(c * DH, DH), DH)
        v_at = pl.ds(pl.multiple_of(w + c * DH, DH), DH)
        q_c, g_c = qcat[c], gcat[c]

        def score(n, top):
            lanes = pl.ds(pl.multiple_of(n * KT, KT), KT)
            k = kvt[k_at, lanes]
            t = jnp.dot(
                q_c, jnp.concatenate([k, k], axis=0), preferred_element_type=F32
            ) + b2_ref[:, lanes]
            t_ref[:, lanes] = t
            for u in range(KT // 128):
                top = jnp.maximum(top, t[:, u * 128 : (u + 1) * 128])
            return top

        top = lax.fori_loop(0, tiles, score, jnp.full((R, 128), -3.0e38, F32))
        top = jnp.max(top, axis=1, keepdims=True)

        def power(n, total):
            lanes = pl.ds(pl.multiple_of(n * KT, KT), KT)
            p = jnp.exp2(t_ref[:, lanes] - top)
            t_ref[:, lanes] = p
            for u in range(KT // 128):
                total = total + p[:, u * 128 : (u + 1) * 128]
            return total

        total = lax.fori_loop(0, tiles, power, jnp.zeros((R, 128), F32))
        inverse = 1.0 / jnp.sum(total, axis=1, keepdims=True)
        qt_c, gt_c = qt[k_at, :], gt[k_at, :]

        def grads(n, dq):
            lanes = pl.ds(pl.multiple_of(n * KT, KT), KT)
            dp = jnp.dot(
                g_c,
                jnp.concatenate([kvt[v_at, lanes], minus], axis=0),
                preferred_element_type=F32,
            )
            weights = t_ref[:, lanes] * inverse
            dl = weights * dp
            db_ref[:, lanes] += dl
            w_half, dl_half = weights.astype(BF), dl.astype(BF)
            acc[k_at, lanes] = jnp.dot(qt_c, dl_half, preferred_element_type=F32) * SCALE
            acc[v_at, lanes] = jnp.dot(gt_c, w_half, preferred_element_type=F32)
            return dq + lax.dot_general(dl_half, kvt[:w, lanes], NT, preferred_element_type=F32)

        dq = lax.fori_loop(0, tiles, grads, jnp.zeros((R, w), F32))
        mine = iota((R, w), 1) // DH == c
        dq_acc[...] += jnp.where(mine, dq, 0.0)
        return 0

    lax.fori_loop(0, cols, column, 0)
    dq_out[...] = (dq_acc[...] * SCALE).astype(BF).reshape(4, rows, w)
    for n in range(4):
        part = acc[:, n * 8 * rows : (n + 1) * 8 * rows].T[:, : 2 * w].astype(BF)
        kn[n * 8 : (n + 1) * 8] = part.reshape(8, rows, 2 * w)
    for s in range(NZ):
        for f in range(4):
            dkv_out[s, f] = kn[natural(s, f)]
    if last:
        x, l = pos_ref[3], pos_ref[4]
        for xs in range(NX):
            for fl in range(NL):
                block = ((x + xs) % NX) * NL + (l ^ fl)
                lanes = pl.ds(pl.multiple_of(block * keys, keys), keys)
                for fy in range(2):
                    f = fy * 2
                    own_out[xs, fl, fy] = db_ref[f * rows : (f + 1) * rows, lanes]
                    other_out[xs, fl, fy] = db_ref[
                        (f + 1) * rows : (f + 2) * rows, lanes
                    ].astype(BF)


def attn(pos, rows, keys, cols, first, last, qgo, kv, b2, db):
    R, tokens, w = 4 * rows, 32 * rows, cols * DH
    wide = -(-2 * w // 128) * 128
    outs = [
        jax.ShapeDtypeStruct((4, rows, w), BF),
        jax.ShapeDtypeStruct((NZ, 4, rows, 2 * w), BF),
    ]
    scratch = [
        pltpu.VMEM((32, rows, 2 * w), BF),
        pltpu.VMEM((2 * w, tokens), BF),
        pltpu.VMEM((cols, R, 2 * DH), BF),
        pltpu.VMEM((cols, R, 3 * DH), BF),
        pltpu.VMEM((w, R), BF),
        pltpu.VMEM((w, R), BF),
        pltpu.VMEM((R, tokens), F32),
        pltpu.VMEM((wide, tokens), F32),
        pltpu.VMEM((R, w), F32),
    ]
    if last:
        outs.append(jax.ShapeDtypeStruct((NX, NL, NY, rows, keys), F32))
        outs.append(jax.ShapeDtypeStruct((NX, NL, NY, rows, keys), BF))
        scratch.append(pltpu.VMEM((R, tokens), F32))
    else:
        outs.append(jax.ShapeDtypeStruct((R, tokens), F32))
    extra = [] if first else [db]
    return pl.pallas_call(
        functools.partial(attn_kernel, rows, keys, cols, first, last),
        in_specs=[SMEM] + [VMEM] * (13 + len(extra)),
        out_specs=[VMEM] * len(outs),
        out_shape=outs,
        scratch_shapes=scratch,
        compiler_params=PARAMS,
        cost_estimate=pl.CostEstimate(
            flops=10 * R * tokens * cols * DH, bytes_accessed=10 * R * tokens, transcendentals=R * tokens * cols
        ),
        name="attn",
    )(pos, *qgo, *kv, b2, *extra)


def per_device(
    queries, key_rows, value_rows, saved_output, grad_output, pair_bias, chain_id, allowed_pairs
):
    rows, width = queries.shape
    keys = pair_bias.shape[2]
    row_index = lax.axis_index("row")
    col_index = lax.axis_index("col")
    y, z, c = row_index // (NZ * NC), (row_index // NC) % NZ, row_index % NC
    me = y * 2 + c
    pos = jnp.stack([me, y, z, col_index // NL, col_index % NL]).astype(jnp.int32)

    flips = ((0, 0), (0, 1), (1, 0), (1, 1))
    pieces = split(pos, (queries, key_rows, value_rows, saved_output, grad_output))
    n_chunks = len(CHUNKS)
    kv_all, qgo_all = [], []
    for n in range(n_chunks):
        mine, got = [], []
        for f, (fy, fc) in enumerate(flips):
            kv, qgo = pieces[2 * (f * n_chunks + n)], pieces[2 * (f * n_chunks + n) + 1]
            mine.append(kv if f == 0 else row_move(kv, fy, 0, fc))
            got.append(qgo if f == 0 else row_move(qgo, fy, 0, fc))
        own = jnp.stack(mine)
        blocks = [None] * NZ
        blocks[0] = own
        up = down = own
        for s in range(1, NZ // 2 + 1):
            up = row_move(up, 0, 1, 0)
            blocks[NZ - s] = up
            if s < NZ // 2:
                down = row_move(down, 0, -1, 0)
                blocks[s] = down
        kv_all.append(blocks)
        qgo_all.append(got)

    labels = jnp.arange(allowed_pairs.shape[0], dtype=jnp.int32)
    groups = chain_id.reshape(NY, NZ, NC, rows)
    groups = lax.dynamic_index_in_dim(groups, z, 1, keepdims=False)
    groups = jnp.stack(
        [
            lax.dynamic_slice(groups, (y ^ fy, c ^ fc, 0), (1, 1, rows)).reshape(rows)
            for fy, fc in flips
        ]
    ).reshape(4 * rows)
    reach = jnp.dot(
        (groups[:, None] == labels[None, :]).astype(F32), (allowed_pairs == 1).astype(F32)
    ).astype(BF)
    bias_own = lax.dynamic_index_in_dim(pair_bias, y, 0, keepdims=False)
    bias_other = lax.dynamic_index_in_dim(pair_bias, 1 - y, 0, keepdims=False)
    bias_own = jnp.stack([bias_own, row_move(bias_other, 1, 0, 0)])
    bias_own = jnp.stack([bias_own, col_move(bias_own, 0, 1)])
    bias_x = [bias_own] + [col_move(bias_own, -xs, 0) for xs in range(1, NX)]
    bias_c = [row_move(part, 0, 0, 1) for part in bias_x]
    b2 = pl.pallas_call(
        functools.partial(bias_kernel, rows, keys),
        in_specs=[SMEM] + [VMEM] * 10,
        out_specs=VMEM,
        out_shape=jax.ShapeDtypeStruct((4 * rows, 32 * rows), F32),
        compiler_params=PARAMS,
        name="bias",
    )(pos, reach, chain_id.reshape(1, -1), *bias_x, *bias_c)

    db = None
    dq_back, dkv_back = [[None] * n_chunks for _ in range(4)], [[None] * n_chunks for _ in range(4)]
    for n, cols in enumerate(CHUNKS):
        first, last = n == 0, n == n_chunks - 1
        out = attn(pos, rows, keys, cols, first, last, qgo_all[n], kv_all[n], b2, db)
        dq, dkv = out[0], out[1]
        if last:
            db_own, db_other = out[2:]
        else:
            db = out[2]
        up = dkv[NZ // 2]
        for s in range(NZ // 2, 1, -1):
            up = (row_move(up, 0, 1, 0).astype(F32) + dkv[s - 1].astype(F32)).astype(BF)
        down = dkv[NZ // 2 + 1]
        for s in range(NZ // 2 - 1, 1, -1):
            down = (row_move(down, 0, -1, 0).astype(F32) + dkv[NZ - s + 1].astype(F32)).astype(BF)
        summed = (
            row_move(up, 0, 1, 0).astype(F32)
            + row_move(down, 0, -1, 0).astype(F32)
            + dkv[0].astype(F32)
        ).astype(BF)
        for f, (fy, fc) in enumerate(flips):
            dq_back[f][n] = dq[f] if f == 0 else row_move(dq[f], fy, 0, fc)
            dkv_back[f][n] = summed[f] if f == 0 else row_move(summed[f], fy, 0, fc)

    db_sum = (db_own + row_move(db_other, 0, 0, 1).astype(F32)).astype(BF)
    total = db_sum[0].astype(F32)
    for xs in range(1, NX):
        total = total + col_move(db_sum[xs], xs, 0).astype(F32)
    total = total[0] + col_move(total[1].astype(BF), 0, 1).astype(F32)
    total = total.astype(BF)
    got = row_move(total[1], 1, 0, 0)
    grad_bias = jnp.where(
        y == 0, jnp.stack([total[0], got]), jnp.stack([got, total[0]])
    )
    grad_q, grad_k, grad_v = join(
        pos, rows, width, [p for f in dq_back for p in f], [p for f in dkv_back for p in f]
    )
    return grad_q, grad_k, grad_v, grad_bias


def solution(mesh):
    whole = P("row", "col")
    bias = P(None, "row", "col")
    return jax.shard_map(
        per_device,
        mesh=mesh,
        in_specs=(whole,) * 5 + (bias, P(), P()),
        out_specs=(whole, whole, whole, bias),
        check_vma=False,
    )
```

```python
import functools
import math

import jax
import jax.numpy as jnp
from jax import lax
from jax.experimental import pallas as pl
from jax.experimental.pallas import tpu as pltpu
from jax.sharding import PartitionSpec as P

H = 2
DH = 32
SCALE = 1.0 / math.sqrt(DH)
LOG2E = math.log2(math.e)
MASKED = -1000000000.0 * LOG2E
NY, NZ, NC = 2, 8, 2
NX, NL = 4, 2
HALF = 7

F32 = jnp.float32
BF = jnp.bfloat16
NT = (((1,), (1,)), ((), ()))
VMEM = pl.BlockSpec(memory_space=pltpu.VMEM)
SMEM = pl.BlockSpec(memory_space=pltpu.SMEM)
ANY = pl.BlockSpec(memory_space=pl.ANY)
PARAMS = pltpu.CompilerParams(vmem_limit_bytes=56 * 2**20)


def iota(shape, dim):
    return lax.broadcasted_iota(jnp.int32, shape, dim)


def row_move(array, dy, dz, dc):
    pairs = []
    for y in range(NY):
        for z in range(NZ):
            for c in range(NC):
                target = ((y ^ dy) * NZ + (z + dz) % NZ) * NC + (c ^ dc)
                pairs.append(((y * NZ + z) * NC + c, target))
    return lax.ppermute(array, "row", pairs)


def col_move(array, dx, dl):
    pairs = []
    for x in range(NX):
        for l in range(NL):
            pairs.append((x * NL + l, ((x + dx) % NX) * NL + (l ^ dl)))
    return lax.ppermute(array, "col", pairs)


def sign(index, half):
    even = 1 - 2 * (index % 2)
    return even if half == 0 else -even


def x_pair(array, half, way):
    pairs = []
    for x in range(NX):
        for l in range(NL):
            pairs.append((x * NL + l, ((x + way * sign(x, half)) % NX) * NL + l))
    return lax.ppermute(array, "col", pairs)


def picks(shape, dim):
    mine = iota(shape, dim)
    distance = iota(shape, 1 - dim) - 2 * mine + (mine & (DH - 1))

    def pick(owner):
        return (distance == (owner % 2) * (HALF * H * DH) + (owner // 2) * DH).astype(BF)

    return pick


def split_kernel(count, me_ref, *refs):
    ins, outs = refs[:count], refs[-4:]
    width = ins[0].shape[1]
    w = HALF * DH
    pick = picks((width, w), 1)
    for f in range(4):
        chosen = pick(me_ref[0] ^ f)
        for u in range(count):
            outs[f][:, u * w : (u + 1) * w] = jnp.dot(
                ins[u][...], chosen, preferred_element_type=F32
            ).astype(BF)


def split(pos, arrays, *after):
    rows = arrays[0].shape[0]
    return pl.pallas_call(
        functools.partial(split_kernel, len(arrays)),
        in_specs=[SMEM] + [VMEM] * len(arrays) + [ANY] * len(after),
        out_specs=[VMEM] * 4,
        out_shape=[jax.ShapeDtypeStruct((rows, len(arrays) * HALF * DH), BF)] * 4,
        compiler_params=PARAMS,
        name="split",
    )(pos, *arrays, *after)


def swap(parts):
    return [
        part if f == 0 else row_move(part, f // 2, 0, f % 2) for f, part in enumerate(parts)
    ]


def join_kernel(count, me_ref, *refs):
    parts, outs = refs[:4], refs[-count:]
    rows, width = outs[0].shape
    w = HALF * DH
    pick = picks((w, width), 0)
    sums = [jnp.zeros((rows, width), F32)] * count
    for f in range(4):
        chosen = pick(me_ref[0] ^ f)
        for u in range(count):
            sums[u] = sums[u] + jnp.dot(
                parts[f][:, u * w : (u + 1) * w], chosen, preferred_element_type=F32
            )
    for u in range(count):
        outs[u][...] = sums[u].astype(BF)


def join(pos, width, parts, count):
    rows = parts[0].shape[0]
    return pl.pallas_call(
        functools.partial(join_kernel, count),
        in_specs=[SMEM] + [VMEM] * 4,
        out_specs=[VMEM] * count,
        out_shape=[jax.ShapeDtypeStruct((rows, width), BF)] * count,
        compiler_params=PARAMS,
        name="join",
    )(pos, *parts)


def turn_in_kernel(pos_ref, *refs):
    parts, out = refs[:4], refs[-1]
    me = pos_ref[0]
    rows, width = parts[0].shape
    blocks = refs[-2]
    for f in range(4):
        blocks[me ^ f] = parts[f][...]
    del refs
    eye = (iota((width, width), 0) == iota((width, width), 1)).astype(BF)
    out[...] = lax.dot_general(
        eye, blocks[...].reshape(4 * rows, width), NT, preferred_element_type=F32
    ).astype(BF)


def turn_in(pos, parts):
    rows, width = parts[0].shape
    return pl.pallas_call(
        lambda pos_ref, *refs: turn_in_kernel(pos_ref, *refs[:4], refs[5], refs[4]),
        in_specs=[SMEM] + [VMEM] * 4,
        out_specs=VMEM,
        out_shape=jax.ShapeDtypeStruct((width, 4 * rows), BF),
        scratch_shapes=[pltpu.VMEM((4, rows, width), BF)],
        compiler_params=PARAMS,
        name="turn_in",
    )(pos, *parts)


def turn_out_kernel(pos_ref, in_ref, *refs):
    outs, blocks = refs[-5:-1], refs[-1]
    me = pos_ref[0]
    width, total = in_ref.shape
    eye = (iota((total, total), 0) == iota((total, total), 1)).astype(BF)
    turned = lax.dot_general(eye, in_ref[...], NT, preferred_element_type=F32).astype(BF)
    blocks[...] = turned.reshape(4, total // 4, width)
    for f in range(4):
        outs[f][...] = blocks[me ^ f]


def turn_out(pos, array, *after):
    width, total = array.shape
    return pl.pallas_call(
        turn_out_kernel,
        in_specs=[SMEM, VMEM] + [ANY] * len(after),
        out_specs=[VMEM] * 4,
        out_shape=[jax.ShapeDtypeStruct((total // 4, width), BF)] * 4,
        scratch_shapes=[pltpu.VMEM((4, total // 4, width), BF)],
        compiler_params=PARAMS,
        name="turn_out",
    )(pos, array, *after)


def exchange_slot(pos_ref, block, fy):
    x, l = pos_ref[3], pos_ref[4]
    d = ((block // NL - x) * sign(x, fy)) & (NX - 1)
    return d ^ (d >> 1), (block % NL) ^ l


def key_lanes(block, rows):
    y, z = block // NX, 2 * (block % NX)
    return [slice(((z + u) * 2 + y) * 2 * rows, ((z + u) * 2 + y + 1) * 2 * rows) for u in (0, 1)]


def bias_kernel(rows, keys, pos_ref, reach_ref, chain_ref, near_ref, far_ref, out_ref):
    for block in range(NX * NL):
        hot = (chain_ref[:, block * keys : (block + 1) * keys] == iota((8, keys), 0)).astype(BF)
        reach = jnp.dot(reach_ref[...], hot, preferred_element_type=F32)
        lanes = key_lanes(block, rows)
        for fy in range(NY):
            n, fl = exchange_slot(pos_ref, block, fy)
            for fc, ref in enumerate((near_ref, far_ref)):
                at = slice((2 * fy + fc) * rows, (2 * fy + fc + 1) * rows)
                value = jnp.where(reach[at] > 0.5, ref[fy, n, fl].astype(F32) * LOG2E, MASKED)
                out_ref[at, lanes[0]] = value[:, : 2 * rows]
                out_ref[at, lanes[1]] = value[:, 2 * rows :]


def attn_kernel(rows, keys, pos_ref, *refs):
    tokens = 32 * rows
    R = 4 * rows
    cols = HALF
    w = cols * DH
    qgo_refs, kv_ref, b2_ref = refs[:4], refs[4], refs[5]
    dq_out, (dkv_out, own_out, other_out), refs = refs[6:10], refs[10:13], refs[13:]
    kvt, b2, qcat, gcat, qt, gt, t_ref, acc, dq_acc, db_ref, in_sem, b2_sem, out_sem = refs
    ins = [
        pltpu.make_async_copy(kv_ref.at[n], kvt.at[:, pl.ds(n * R, R)], in_sem.at[n])
        for n in range(NZ)
    ]
    ins.append(pltpu.make_async_copy(b2_ref, b2, b2_sem))
    for copy in ins:
        copy.start()
    eye_w = (iota((w, w), 0) == iota((w, w), 1)).astype(BF)
    q, g, o = (
        jnp.concatenate(
            [qgo_refs[f][:, u * w : (u + 1) * w] for f in range(4)], axis=0
        )
        for u in range(3)
    )
    qt[...] = lax.dot_general(eye_w, q, NT, preferred_element_type=F32).astype(BF)
    gt[...] = lax.dot_general(eye_w, g, NT, preferred_element_type=F32).astype(BF)
    qs = q.astype(F32) * (SCALE * LOG2E)
    q_hi = qs.astype(BF)
    q_lo = (qs - q_hi.astype(F32)).astype(BF)
    go = g.astype(F32) * o.astype(F32)
    go_hi = go.astype(BF)
    go_lo = (go - go_hi.astype(F32)).astype(BF)
    for c in range(cols):
        d = slice(c * DH, (c + 1) * DH)
        qcat[c] = jnp.concatenate([q_hi[:, d], q_lo[:, d]], axis=1)
        gcat[c] = jnp.concatenate([g[:, d], go_hi[:, d], go_lo[:, d]], axis=1)
    db_ref[...] = jnp.zeros_like(db_ref)
    dq_acc[...] = jnp.zeros_like(dq_acc)
    for copy in ins:
        copy.wait()
    minus = jnp.full((2 * DH, tokens), -1.0, BF)
    tiles = [slice(u, u + 128) for u in range(0, tokens, 128)]

    def column(c, _):
        k_at = pl.ds(pl.multiple_of(c * DH, DH), DH)
        v_at = pl.ds(pl.multiple_of(w + c * DH, DH), DH)
        k = kvt[k_at, :]
        t = jnp.dot(qcat[c], jnp.concatenate([k, k], axis=0), preferred_element_type=F32)
        t = t + b2[...]
        t_ref[...] = t
        top = t[:, tiles[0]]
        for tile in tiles[1:]:
            top = jnp.maximum(top, t[:, tile])
        p = jnp.exp2(t_ref[...] - jnp.max(top, axis=1, keepdims=True))
        t_ref[...] = p
        total = p[:, tiles[0]]
        for tile in tiles[1:]:
            total = total + p[:, tile]
        inverse = 1.0 / jnp.sum(total, axis=1, keepdims=True)
        dp = jnp.dot(
            gcat[c], jnp.concatenate([kvt[v_at, :], minus], axis=0), preferred_element_type=F32
        )
        weights = t_ref[...] * inverse
        dl = weights * dp
        db_ref[...] += dl
        w_half, dl_half = weights.astype(BF), dl.astype(BF)
        dk = jnp.dot(qt[k_at, :], dl_half, preferred_element_type=F32) * SCALE
        acc[k_at, :] = dk.astype(BF)
        dv = jnp.dot(gt[k_at, :], w_half, preferred_element_type=F32)
        acc[v_at, :] = dv.astype(BF)
        dq = lax.dot_general(dl_half, kvt[:w, :], NT, preferred_element_type=F32)
        mine = iota((R, w), 1) // DH == c
        dq_acc[...] += jnp.where(mine, dq, 0.0)
        return 0

    lax.fori_loop(0, cols, column, 0)
    for f in range(4):
        dq_out[f][...] = (dq_acc[f * rows : (f + 1) * rows, :] * SCALE).astype(BF)
    outs = [
        pltpu.make_async_copy(acc.at[:, pl.ds(n * R, R)], dkv_out.at[n], out_sem.at[n])
        for n in range(NZ)
    ]
    for copy in outs:
        copy.start()
    for block in range(NX * NL):
        lanes = key_lanes(block, rows)
        for fy in range(NY):
            n, fl = exchange_slot(pos_ref, block, fy)
            for fc, out in enumerate((own_out, other_out)):
                at = slice((2 * fy + fc) * rows, (2 * fy + fc + 1) * rows)
                part = jnp.concatenate([db_ref[at, lanes[0]], db_ref[at, lanes[1]]], axis=1)
                out[fy, n, fl] = part.astype(out.dtype)
    for copy in outs:
        copy.wait()


def attn(pos, rows, keys, qgo, kv, b2):
    cols = HALF
    R, tokens, w = 4 * rows, 32 * rows, cols * DH
    outs = [
        *[jax.ShapeDtypeStruct((rows, w), BF)] * 4,
        jax.ShapeDtypeStruct((NZ, 2 * w, R), BF),
        jax.ShapeDtypeStruct((NY, NX, NL, rows, keys), F32),
        jax.ShapeDtypeStruct((NY, NX, NL, rows, keys), BF),
    ]
    scratch = [
        pltpu.VMEM((2 * w, tokens), BF),
        pltpu.VMEM((R, tokens), F32),
        pltpu.VMEM((cols, R, 2 * DH), BF),
        pltpu.VMEM((cols, R, 3 * DH), BF),
        pltpu.VMEM((w, R), BF),
        pltpu.VMEM((w, R), BF),
        pltpu.VMEM((R, tokens), F32),
        pltpu.VMEM((2 * w, tokens), BF),
        pltpu.VMEM((R, w), F32),
        pltpu.VMEM((R, tokens), F32),
        pltpu.SemaphoreType.DMA((NZ,)),
        pltpu.SemaphoreType.DMA,
        pltpu.SemaphoreType.DMA((NZ,)),
    ]
    ins = [*qgo, kv, b2]
    return pl.pallas_call(
        functools.partial(attn_kernel, rows, keys),
        in_specs=[SMEM] + [VMEM] * 4 + [ANY] * 2,
        out_specs=[VMEM] * 4 + [ANY] + [VMEM] * 2,
        out_shape=outs,
        scratch_shapes=scratch,
        compiler_params=PARAMS,
        cost_estimate=pl.CostEstimate(
            flops=9 * 10**9 * cols, bytes_accessed=10 * R * tokens, transcendentals=R * tokens * cols
        ),
        name="attn",
    )(pos, *ins)


def per_device(
    queries, key_rows, value_rows, saved_output, grad_output, pair_bias, chain_id, allowed_pairs
):
    rows, width = queries.shape
    keys = pair_bias.shape[2]
    row_index = lax.axis_index("row")
    col_index = lax.axis_index("col")
    y, z, c = row_index // (NZ * NC), (row_index // NC) % NZ, row_index % NC
    me = y * 2 + c
    pos = jnp.stack([me, y, z, col_index // NL, col_index % NL]).astype(jnp.int32)

    groups = [
        [(y * NZ + z) * NC + c for z in range(NZ)] for y in range(NY) for c in range(NC)
    ]
    bias_own = lax.dynamic_index_in_dim(pair_bias, y, 0, keepdims=False)
    bias_other = lax.dynamic_index_in_dim(pair_bias, 1 - y, 0, keepdims=False)
    bias_rows = (bias_own, row_move(bias_other, 1, 0, 0))

    kv_parts = swap(split(pos, (key_rows, value_rows)))
    kv = lax.all_gather(turn_in(pos, kv_parts), "row", axis_index_groups=groups)
    rest = swap(split(pos, (queries, grad_output, saved_output), kv_parts[3]))

    labels = jnp.arange(allowed_pairs.shape[0], dtype=jnp.int32)
    chains = chain_id.reshape(NY, NZ, NC, rows)
    chains = lax.dynamic_index_in_dim(chains, z, 1, keepdims=False)
    chains = jnp.stack(
        [
            lax.dynamic_slice(chains, (y ^ fy, c ^ fc, 0), (1, 1, rows)).reshape(rows)
            for fy, fc in ((0, 0), (0, 1), (1, 0), (1, 1))
        ]
    ).reshape(4 * rows)
    reach = jnp.dot(
        (chains[:, None] == labels[None, :]).astype(F32), (allowed_pairs == 1).astype(F32)
    ).astype(BF)
    bias_lanes = col_move(jnp.stack(bias_rows), 0, 1)
    bias_near = []
    for fy in range(NY):
        own = jnp.stack([bias_rows[fy], bias_lanes[fy]])
        both = jnp.stack([own, x_pair(own, fy, 1)])
        bias_near += [both, x_pair(both, fy, -1)]
    bias_near = jnp.stack([jnp.concatenate(bias_near[:2]), jnp.concatenate(bias_near[2:])])
    bias_far = row_move(bias_near, 0, 0, 1)
    b2 = pl.pallas_call(
        functools.partial(bias_kernel, rows, keys),
        in_specs=[SMEM] + [VMEM] * 4,
        out_specs=VMEM,
        out_shape=jax.ShapeDtypeStruct((4 * rows, 32 * rows), F32),
        compiler_params=PARAMS,
        name="bias",
    )(pos, reach, chain_id.reshape(1, -1), bias_near, bias_far)

    *dq, dkv, db_own, db_other = attn(pos, rows, keys, rest, kv, b2)
    summed = lax.psum_scatter(
        dkv.reshape(NZ * 2 * HALF * DH, 4 * rows),
        "row",
        scatter_dimension=0,
        axis_index_groups=groups,
        tiled=True,
    )
    (grad_q,) = join(pos, width, swap(dq), 1)

    db_sum = (db_own + row_move(db_other, 0, 0, 1).astype(F32)).astype(BF)
    total = []
    for fy in range(NY):
        part = x_pair(db_sum[fy, 2:], fy, -1).astype(F32) + db_sum[fy, :2].astype(F32)
        total.append(part[0] + x_pair(part[1].astype(BF), fy, 1).astype(F32))
    total = jnp.stack(total)
    total = total[:, 0] + col_move(total[:, 1].astype(BF), 0, 1).astype(F32)
    total = total.astype(BF)
    got = row_move(total[1], 1, 0, 0)
    grad_bias = jnp.where(
        y == 0, jnp.stack([total[0], got]), jnp.stack([got, total[0]])
    )
    back = swap(turn_out(pos, summed, grad_q, grad_bias))
    grad_k, grad_v = join(pos, width, back, 2)
    return grad_q, grad_k, grad_v, grad_bias


def solution(mesh):
    whole = P("row", "col")
    bias = P(None, "row", "col")
    return jax.shard_map(
        per_device,
        mesh=mesh,
        in_specs=(whole,) * 5 + (bias, P(), P()),
        out_specs=(whole, whole, whole, bias),
        check_vma=False,
    )
```

```python
import functools
import math

import jax
import jax.numpy as jnp
from jax import lax
from jax.experimental import pallas as pl
from jax.experimental.pallas import tpu as pltpu
from jax.sharding import PartitionSpec as P

H = 2
DH = 32
SCALE = 1.0 / math.sqrt(DH)
LOG2E = math.log2(math.e)
MASKED = -1000000000.0 * LOG2E
NY, NZ, NC = 2, 8, 2
NX, NL = 4, 2
HALF = 7
BLOCK = 128
PART = 3072

F32 = jnp.float32
BF = jnp.bfloat16
NT = (((1,), (1,)), ((), ()))
VMEM = pl.BlockSpec(memory_space=pltpu.VMEM)
SMEM = pl.BlockSpec(memory_space=pltpu.SMEM)
ANY = pl.BlockSpec(memory_space=pl.ANY)
PARAMS = pltpu.CompilerParams(vmem_limit_bytes=56 * 2**20)


def iota(shape, dim):
    return lax.broadcasted_iota(jnp.int32, shape, dim)


def row_move(array, dy, dz, dc):
    pairs = []
    for y in range(NY):
        for z in range(NZ):
            for c in range(NC):
                target = ((y ^ dy) * NZ + (z + dz) % NZ) * NC + (c ^ dc)
                pairs.append(((y * NZ + z) * NC + c, target))
    return lax.ppermute(array, "row", pairs)


def col_move(array, dx, dl):
    pairs = []
    for x in range(NX):
        for l in range(NL):
            pairs.append((x * NL + l, ((x + dx) % NX) * NL + (l ^ dl)))
    return lax.ppermute(array, "col", pairs)


def sign(index, half):
    even = 1 - 2 * (index % 2)
    return even if half == 0 else -even


def x_pair(array, half, way):
    pairs = []
    for x in range(NX):
        for l in range(NL):
            pairs.append((x * NL + l, ((x + way * sign(x, half)) % NX) * NL + l))
    return lax.ppermute(array, "col", pairs)


def picks(shape, dim):
    mine = iota(shape, dim)
    distance = iota(shape, 1 - dim) - 2 * mine + (mine & (DH - 1))

    def pick(owner):
        return (distance == (owner % 2) * (HALF * H * DH) + (owner // 2) * DH).astype(BF)

    return pick


def split_kernel(count, flips, *refs):
    ins, outs = refs[:count], refs[-len(flips) :]
    row = lax.axis_index("row")
    me = (row // (NZ * NC)) * 2 + row % NC
    width = ins[0].shape[1]
    w = HALF * DH
    pick = picks((width, w), 1)
    for out, f in zip(outs, flips):
        chosen = pick(me ^ f)
        for u in range(count):
            out[:, u * w : (u + 1) * w] = jnp.dot(
                ins[u][...], chosen, preferred_element_type=F32
            ).astype(BF)


def split(flips, arrays, *after):
    rows = arrays[0].shape[0]
    return pl.pallas_call(
        functools.partial(split_kernel, len(arrays), flips),
        in_specs=[VMEM] * len(arrays) + [ANY] * len(after),
        out_specs=[VMEM] * len(flips),
        out_shape=[jax.ShapeDtypeStruct((rows, len(arrays) * HALF * DH), BF)] * len(flips),
        compiler_params=PARAMS,
        name="split",
    )(*arrays, *after)


def swap(parts):
    return [
        part if f == 0 else row_move(part, f // 2, 0, f % 2) for f, part in enumerate(parts)
    ]


def join_kernel(count, me_ref, *refs):
    parts, outs = refs[:4], refs[-count:]
    rows, width = outs[0].shape
    w = HALF * DH
    pick = picks((w, width), 0)
    sums = [jnp.zeros((rows, width), F32)] * count
    for f in range(4):
        chosen = pick(me_ref[0] ^ f)
        for u in range(count):
            sums[u] = sums[u] + jnp.dot(
                parts[f][:, u * w : (u + 1) * w], chosen, preferred_element_type=F32
            )
    for u in range(count):
        outs[u][...] = sums[u].astype(BF)


def join(pos, width, parts, count):
    rows = parts[0].shape[0]
    return pl.pallas_call(
        functools.partial(join_kernel, count),
        in_specs=[SMEM] + [VMEM] * 4,
        out_specs=[VMEM] * count,
        out_shape=[jax.ShapeDtypeStruct((rows, width), BF)] * count,
        compiler_params=PARAMS,
        name="join",
    )(pos, *parts)


def turn_in_kernel(pos_ref, *refs):
    parts, out = refs[:4], refs[-1]
    me = pos_ref[0]
    rows, width = parts[0].shape
    blocks = refs[-2]
    for f in range(4):
        blocks[me ^ f] = parts[f][...]
    del refs
    eye = (iota((width, width), 0) == iota((width, width), 1)).astype(BF)
    out[...] = lax.dot_general(
        eye, blocks[...].reshape(4 * rows, width), NT, preferred_element_type=F32
    ).astype(BF)


def turn_in(pos, parts):
    rows, width = parts[0].shape
    return pl.pallas_call(
        lambda pos_ref, *refs: turn_in_kernel(pos_ref, *refs[:4], refs[5], refs[4]),
        in_specs=[SMEM] + [VMEM] * 4,
        out_specs=VMEM,
        out_shape=jax.ShapeDtypeStruct((width, 4 * rows), BF),
        scratch_shapes=[pltpu.VMEM((4, rows, width), BF)],
        compiler_params=PARAMS,
        name="turn_in",
    )(pos, *parts)


def turn_out_kernel(pos_ref, in_ref, *refs):
    outs, blocks = refs[-5:-1], refs[-1]
    me = pos_ref[0]
    width, total = in_ref.shape
    eye = (iota((total, total), 0) == iota((total, total), 1)).astype(BF)
    turned = lax.dot_general(eye, in_ref[...], NT, preferred_element_type=F32).astype(BF)
    blocks[...] = turned.reshape(4, total // 4, width)
    for f in range(4):
        outs[f][...] = blocks[me ^ f]


def turn_out(pos, array, *after):
    width, total = array.shape
    return pl.pallas_call(
        turn_out_kernel,
        in_specs=[SMEM, VMEM] + [ANY] * len(after),
        out_specs=[VMEM] * 4,
        out_shape=[jax.ShapeDtypeStruct((total // 4, width), BF)] * 4,
        scratch_shapes=[pltpu.VMEM((4, total // 4, width), BF)],
        compiler_params=PARAMS,
        name="turn_out",
    )(pos, array, *after)


def exchange_slot(pos_ref, block, fy):
    x, l = pos_ref[3], pos_ref[4]
    d = ((block // NL - x) * sign(x, fy)) & (NX - 1)
    return d ^ (d >> 1), (block % NL) ^ l


def key_lanes(block, rows):
    y, z = block // NX, 2 * (block % NX)
    return [slice(((z + u) * 2 + y) * 2 * rows, ((z + u) * 2 + y + 1) * 2 * rows) for u in (0, 1)]


def bias_kernel(rows, keys, pos_ref, reach_ref, chain_ref, near_ref, far_ref, out_ref):
    for block in range(NX * NL):
        hot = (chain_ref[:, block * keys : (block + 1) * keys] == iota((8, keys), 0)).astype(BF)
        reach = jnp.dot(reach_ref[...], hot, preferred_element_type=F32)
        lanes = key_lanes(block, rows)
        for fy in range(NY):
            n, fl = exchange_slot(pos_ref, block, fy)
            for fc, ref in enumerate((near_ref, far_ref)):
                at = slice((2 * fy + fc) * rows, (2 * fy + fc + 1) * rows)
                value = jnp.where(reach[at] > 0.5, ref[fy, n, fl].astype(F32) * LOG2E, MASKED)
                out_ref[at, lanes[0]] = value[:, : 2 * rows]
                out_ref[at, lanes[1]] = value[:, 2 * rows :]


def attn_kernel(rows, keys, pos_ref, *refs):
    tokens = 32 * rows
    R = 4 * rows
    cols = HALF
    w = cols * DH
    qgo_refs, kv_ref, b2_ref = refs[:4], refs[4], refs[5]
    dq_out, (dkv_out, own_out, other_out), refs = refs[6:10], refs[10:13], refs[13:]
    kvt, b2, qcat, gcat, qt, gt, t_ref, acc, sums, dq_acc, db_ref, in_sem, b2_sem, out_sem = refs
    ins = [
        pltpu.make_async_copy(kv_ref.at[n], kvt.at[:, pl.ds(n * R, R)], in_sem.at[n])
        for n in range(NZ)
    ]
    ins.append(pltpu.make_async_copy(b2_ref, b2, b2_sem))
    for copy in ins:
        copy.start()
    eye_w = (iota((w, w), 0) == iota((w, w), 1)).astype(BF)
    q, g, o = (
        jnp.concatenate(
            [qgo_refs[f][:, u * w : (u + 1) * w] for f in range(4)], axis=0
        )
        for u in range(3)
    )
    qt[...] = lax.dot_general(eye_w, q, NT, preferred_element_type=F32).astype(BF)
    gt[...] = lax.dot_general(eye_w, g, NT, preferred_element_type=F32).astype(BF)
    qs = q.astype(F32) * (SCALE * LOG2E)
    q_hi = qs.astype(BF)
    q_lo = (qs - q_hi.astype(F32)).astype(BF)
    go = g.astype(F32) * o.astype(F32)
    go_hi = go.astype(BF)
    go_lo = (go - go_hi.astype(F32)).astype(BF)
    for c in range(cols):
        d = slice(c * DH, (c + 1) * DH)
        qcat[c] = jnp.concatenate([q_hi[:, d], q_lo[:, d]], axis=1)
        gcat[c] = jnp.concatenate([g[:, d], go_hi[:, d], go_lo[:, d]], axis=1)
    db_ref[...] = jnp.zeros_like(db_ref)
    for copy in ins:
        copy.wait()
    minus = jnp.full((2 * DH, PART), -1.0, BF)
    per_column = R // BLOCK
    blocks = cols * per_column
    parts = [slice(u, u + PART) for u in range(0, tokens, PART)]

    def fold(combine, running, array):
        for u in range(0, PART, 128):
            running = combine(running, array[:, u : u + 128])
        return running

    def places(i):
        c, r = i // per_column, i % per_column
        return (
            c,
            pl.ds(pl.multiple_of(c * DH, DH), DH),
            pl.ds(pl.multiple_of(w + c * DH, DH), DH),
            pl.ds(pl.multiple_of(r * BLOCK, BLOCK), BLOCK),
            r,
        )

    def score(i, slot, part, top):
        c, k_at, _, at, _ = places(i)
        k = kvt[k_at, part]
        t = jnp.dot(qcat[c, at, :], jnp.concatenate([k, k], axis=0), preferred_element_type=F32)
        t = t + b2[at, part]
        t_ref[slot, :, part] = t
        return fold(jnp.maximum, top, t)

    def power(slot, part, top, total):
        p = jnp.exp2(t_ref[slot, :, part] - top)
        t_ref[slot, :, part] = p
        return fold(jnp.add, total, p)

    def grads(i, part, inverse, dq):
        c, k_at, v_at, at, r = places(i)
        v = jnp.concatenate([kvt[v_at, part], minus], axis=0)
        dp = jnp.dot(gcat[c, at, :], v, preferred_element_type=F32)
        weights = t_ref[i % 3, :, part] * inverse
        dl = weights * dp
        db_ref[at, part] += dl
        w_half, dl_half = weights.astype(BF), dl.astype(BF)
        dk = jnp.dot(qt[k_at, at], dl_half, preferred_element_type=F32)
        dv = jnp.dot(gt[k_at, at], w_half, preferred_element_type=F32)
        dk = jnp.where(r == 0, 0.0, sums[0, :, part]) + dk
        dv = jnp.where(r == 0, 0.0, sums[1, :, part]) + dv
        sums[0, :, part] = dk
        sums[1, :, part] = dv
        acc[k_at, part] = (dk * SCALE).astype(BF)
        acc[v_at, part] = dv.astype(BF)
        return dq + lax.dot_general(dl_half, kvt[k_at, part], NT, preferred_element_type=F32)

    lowest = jnp.full((BLOCK, 128), -3.0e38, F32)
    zero = jnp.zeros((BLOCK, 128), F32)

    def highest(top):
        return jnp.max(top, axis=1, keepdims=True)

    def inverted(total):
        return 1.0 / jnp.sum(total, axis=1, keepdims=True)

    top0, top1, total0 = lowest, lowest, zero
    for part in parts:
        top0 = score(0, 0, part, top0)
    top0 = highest(top0)
    for part in parts:
        total0 = power(0, part, top0, total0)
        top1 = score(1, 1, part, top1)

    def step(i, carry):
        top, inverse = carry
        later = jnp.minimum(i + 2, blocks - 1)
        new_top, total, dq = lowest, zero, jnp.zeros((BLOCK, DH), F32)
        for part in parts:
            dq = grads(i, part, inverse, dq)
            total = power((i + 1) % 3, part, top, total)
            new_top = score(later, (i + 2) % 3, part, new_top)
        c, _, _, at, _ = places(i)
        dq_acc[c, at, :] = dq
        return highest(new_top), inverted(total)

    lax.fori_loop(0, blocks, step, (highest(top1), inverted(total0)))
    for f in range(4):
        at = slice(f * rows, (f + 1) * rows)
        dq = jnp.concatenate([dq_acc[c, at, :] for c in range(cols)], axis=1)
        dq_out[f][...] = (dq * SCALE).astype(BF)
    outs = [
        pltpu.make_async_copy(acc.at[:, pl.ds(n * R, R)], dkv_out.at[n], out_sem.at[n])
        for n in range(NZ)
    ]
    for copy in outs:
        copy.start()
    for block in range(NX * NL):
        lanes = key_lanes(block, rows)
        for fy in range(NY):
            n, fl = exchange_slot(pos_ref, block, fy)
            for fc, out in enumerate((own_out, other_out)):
                at = slice((2 * fy + fc) * rows, (2 * fy + fc + 1) * rows)
                part = jnp.concatenate([db_ref[at, lanes[0]], db_ref[at, lanes[1]]], axis=1)
                out[fy, n, fl] = part.astype(out.dtype)
    for copy in outs:
        copy.wait()


def attn(pos, rows, keys, qgo, kv, b2):
    cols = HALF
    R, tokens, w = 4 * rows, 32 * rows, cols * DH
    outs = [
        *[jax.ShapeDtypeStruct((rows, w), BF)] * 4,
        jax.ShapeDtypeStruct((NZ, 2 * w, R), BF),
        jax.ShapeDtypeStruct((NY, NX, NL, rows, keys), F32),
        jax.ShapeDtypeStruct((NY, NX, NL, rows, keys), BF),
    ]
    scratch = [
        pltpu.VMEM((2 * w, tokens), BF),
        pltpu.VMEM((R, tokens), F32),
        pltpu.VMEM((cols, R, 2 * DH), BF),
        pltpu.VMEM((cols, R, 3 * DH), BF),
        pltpu.VMEM((w, R), BF),
        pltpu.VMEM((w, R), BF),
        pltpu.VMEM((3, BLOCK, tokens), F32),
        pltpu.VMEM((2 * w, tokens), BF),
        pltpu.VMEM((2, DH, tokens), F32),
        pltpu.VMEM((cols, R, DH), F32),
        pltpu.VMEM((R, tokens), F32),
        pltpu.SemaphoreType.DMA((NZ,)),
        pltpu.SemaphoreType.DMA,
        pltpu.SemaphoreType.DMA((NZ,)),
    ]
    ins = [*qgo, kv, b2]
    return pl.pallas_call(
        functools.partial(attn_kernel, rows, keys),
        in_specs=[SMEM] + [VMEM] * 4 + [ANY] * 2,
        out_specs=[VMEM] * 4 + [ANY] + [VMEM] * 2,
        out_shape=outs,
        scratch_shapes=scratch,
        compiler_params=PARAMS,
        cost_estimate=pl.CostEstimate(
            flops=9 * 10**9 * cols, bytes_accessed=10 * R * tokens, transcendentals=R * tokens * cols
        ),
        name="attn",
    )(pos, *ins)


def per_device(
    queries, key_rows, value_rows, saved_output, grad_output, pair_bias, chain_id, allowed_pairs
):
    rows, width = queries.shape
    keys = pair_bias.shape[2]
    row_index = lax.axis_index("row")
    col_index = lax.axis_index("col")
    y, z, c = row_index // (NZ * NC), (row_index // NC) % NZ, row_index % NC
    me = y * 2 + c
    pos = jnp.stack([me, y, z, col_index // NL, col_index % NL]).astype(jnp.int32)

    groups = [
        [(y * NZ + z) * NC + c for z in range(NZ)] for y in range(NY) for c in range(NC)
    ]
    bias_own = lax.dynamic_index_in_dim(pair_bias, y, 0, keepdims=False)
    bias_other = lax.dynamic_index_in_dim(pair_bias, 1 - y, 0, keepdims=False)
    bias_rows = (bias_own, row_move(bias_other, 1, 0, 0))

    kv_far = split((2, 3), (key_rows, value_rows))
    kv_near = split((0, 1), (key_rows, value_rows), kv_far[0])
    kv_parts = swap([*kv_near, *kv_far])
    kv = lax.all_gather(turn_in(pos, kv_parts), "row", axis_index_groups=groups)
    rest = swap(split((0, 1, 2, 3), (queries, grad_output, saved_output), kv_parts[3]))

    labels = jnp.arange(allowed_pairs.shape[0], dtype=jnp.int32)
    chains = chain_id.reshape(NY, NZ, NC, rows)
    chains = lax.dynamic_index_in_dim(chains, z, 1, keepdims=False)
    chains = jnp.stack(
        [
            lax.dynamic_slice(chains, (y ^ fy, c ^ fc, 0), (1, 1, rows)).reshape(rows)
            for fy, fc in ((0, 0), (0, 1), (1, 0), (1, 1))
        ]
    ).reshape(4 * rows)
    reach = jnp.dot(
        (chains[:, None] == labels[None, :]).astype(F32), (allowed_pairs == 1).astype(F32)
    ).astype(BF)
    bias_lanes = col_move(jnp.stack(bias_rows), 0, 1)
    bias_near = []
    for fy in range(NY):
        own = jnp.stack([bias_rows[fy], bias_lanes[fy]])
        both = jnp.stack([own, x_pair(own, fy, 1)])
        bias_near += [both, x_pair(both, fy, -1)]
    bias_near = jnp.stack([jnp.concatenate(bias_near[:2]), jnp.concatenate(bias_near[2:])])
    bias_far = row_move(bias_near, 0, 0, 1)
    b2 = pl.pallas_call(
        functools.partial(bias_kernel, rows, keys),
        in_specs=[SMEM] + [VMEM] * 4,
        out_specs=VMEM,
        out_shape=jax.ShapeDtypeStruct((4 * rows, 32 * rows), F32),
        compiler_params=PARAMS,
        name="bias",
    )(pos, reach, chain_id.reshape(1, -1), bias_near, bias_far)

    *dq, dkv, db_own, db_other = attn(pos, rows, keys, rest, kv, b2)
    summed = lax.psum_scatter(
        dkv.reshape(NZ * 2 * HALF * DH, 4 * rows),
        "row",
        scatter_dimension=0,
        axis_index_groups=groups,
        tiled=True,
    )
    (grad_q,) = join(pos, width, swap(dq), 1)

    db_sum = (db_own + row_move(db_other, 0, 0, 1).astype(F32)).astype(BF)
    total = []
    for fy in range(NY):
        part = x_pair(db_sum[fy, 2:], fy, -1).astype(F32) + db_sum[fy, :2].astype(F32)
        total.append(part[0] + x_pair(part[1].astype(BF), fy, 1).astype(F32))
    total = jnp.stack(total)
    total = total[:, 0] + col_move(total[:, 1].astype(BF), 0, 1).astype(F32)
    total = total.astype(BF)
    got = row_move(total[1], 1, 0, 0)
    grad_bias = jnp.where(
        y == 0, jnp.stack([total[0], got]), jnp.stack([got, total[0]])
    )
    back = swap(turn_out(pos, summed, grad_q, grad_bias))
    grad_k, grad_v = join(pos, width, back, 2)
    return grad_q, grad_k, grad_v, grad_bias


def solution(mesh):
    whole = P("row", "col")
    bias = P(None, "row", "col")
    return jax.shard_map(
        per_device,
        mesh=mesh,
        in_specs=(whole,) * 5 + (bias, P(), P()),
        out_specs=(whole, whole, whole, bias),
        check_vma=False,
    )
```

```python
import functools
import math

import jax
import jax.numpy as jnp
from jax import lax
from jax.experimental import pallas as pl
from jax.experimental.pallas import tpu as pltpu
from jax.sharding import PartitionSpec as P

H = 2
DH = 32
SCALE = 1.0 / math.sqrt(DH)
LOG2E = math.log2(math.e)
MASKED = -1000000000.0 * LOG2E
NY, NZ, NC = 2, 8, 2
NX, NL = 4, 2
HALF = 7
BLOCK = 128
PART = 3072

F32 = jnp.float32
BF = jnp.bfloat16
NT = (((1,), (1,)), ((), ()))
VMEM = pl.BlockSpec(memory_space=pltpu.VMEM)
SMEM = pl.BlockSpec(memory_space=pltpu.SMEM)
ANY = pl.BlockSpec(memory_space=pl.ANY)
HBM = pl.BlockSpec(memory_space=pltpu.HBM)
SMALL = pltpu.CompilerParams(vmem_limit_bytes=16 * 2**20)
LARGE = pltpu.CompilerParams(vmem_limit_bytes=34 * 2**20)


def iota(shape, dim):
    return lax.broadcasted_iota(jnp.int32, shape, dim)


def row_move(array, dy, dz, dc):
    pairs = []
    for y in range(NY):
        for z in range(NZ):
            for c in range(NC):
                target = ((y ^ dy) * NZ + (z + dz) % NZ) * NC + (c ^ dc)
                pairs.append(((y * NZ + z) * NC + c, target))
    return lax.ppermute(array, "row", pairs)


def col_move(array, dx, dl):
    pairs = []
    for x in range(NX):
        for l in range(NL):
            pairs.append((x * NL + l, ((x + dx) % NX) * NL + (l ^ dl)))
    return lax.ppermute(array, "col", pairs)


def sign(index, half):
    even = 1 - 2 * (index % 2)
    return even if half == 0 else -even


def x_pair(array, half, way):
    pairs = []
    for x in range(NX):
        for l in range(NL):
            pairs.append((x * NL + l, ((x + way * sign(x, half)) % NX) * NL + l))
    return lax.ppermute(array, "col", pairs)


def picks(shape, dim):
    mine = iota(shape, dim)
    distance = iota(shape, 1 - dim) - 2 * mine + (mine & (DH - 1))

    def pick(owner):
        return (distance == (owner % 2) * (HALF * H * DH) + (owner // 2) * DH).astype(BF)

    return pick


def split_kernel(count, flips, *refs):
    ins, outs = refs[:count], refs[-len(flips) :]
    row = lax.axis_index("row")
    me = (row // (NZ * NC)) * 2 + row % NC
    width = ins[0].shape[1]
    w = HALF * DH
    pick = picks((width, w), 1)
    for out, f in zip(outs, flips):
        chosen = pick(me ^ f)
        for u in range(count):
            out[:, u * w : (u + 1) * w] = jnp.dot(
                ins[u][...], chosen, preferred_element_type=F32
            ).astype(BF)


def split(flips, arrays, *after):
    rows = arrays[0].shape[0]
    return pl.pallas_call(
        functools.partial(split_kernel, len(arrays), flips),
        in_specs=[VMEM] * len(arrays) + [ANY] * len(after),
        out_specs=[VMEM] * len(flips),
        out_shape=[jax.ShapeDtypeStruct((rows, len(arrays) * HALF * DH), BF)] * len(flips),
        compiler_params=SMALL,
        name="split",
    )(*arrays, *after)


def swap(parts):
    return [
        part if f == 0 else row_move(part, f // 2, 0, f % 2) for f, part in enumerate(parts)
    ]


def join_kernel(count, me_ref, *refs):
    parts, outs = refs[:4], refs[-count:]
    rows, width = outs[0].shape
    w = HALF * DH
    pick = picks((w, width), 0)
    sums = [jnp.zeros((rows, width), F32)] * count
    for f in range(4):
        chosen = pick(me_ref[0] ^ f)
        for u in range(count):
            sums[u] = sums[u] + jnp.dot(
                parts[f][:, u * w : (u + 1) * w], chosen, preferred_element_type=F32
            )
    for u in range(count):
        outs[u][...] = sums[u].astype(BF)


def join(pos, width, parts, count):
    rows = parts[0].shape[0]
    return pl.pallas_call(
        functools.partial(join_kernel, count),
        in_specs=[SMEM] + [VMEM] * 4,
        out_specs=[VMEM] * count,
        out_shape=[jax.ShapeDtypeStruct((rows, width), BF)] * count,
        compiler_params=SMALL,
        name="join",
    )(pos, *parts)


def turn_in_kernel(pos_ref, *refs):
    parts, out = refs[:4], refs[-1]
    me = pos_ref[0]
    rows, width = parts[0].shape
    blocks = refs[-2]
    for f in range(4):
        blocks[me ^ f] = parts[f][...]
    del refs
    eye = (iota((width, width), 0) == iota((width, width), 1)).astype(BF)
    out[...] = lax.dot_general(
        eye, blocks[...].reshape(4 * rows, width), NT, preferred_element_type=F32
    ).astype(BF)


def turn_in(pos, parts):
    rows, width = parts[0].shape
    return pl.pallas_call(
        lambda pos_ref, *refs: turn_in_kernel(pos_ref, *refs[:4], refs[5], refs[4]),
        in_specs=[SMEM] + [VMEM] * 4,
        out_specs=VMEM,
        out_shape=jax.ShapeDtypeStruct((width, 4 * rows), BF),
        scratch_shapes=[pltpu.VMEM((4, rows, width), BF)],
        compiler_params=SMALL,
        name="turn_in",
    )(pos, *parts)


def turn_out_kernel(pos_ref, in_ref, *refs):
    outs, blocks = refs[-5:-1], refs[-1]
    me = pos_ref[0]
    width, total = in_ref.shape
    eye = (iota((total, total), 0) == iota((total, total), 1)).astype(BF)
    turned = lax.dot_general(eye, in_ref[...], NT, preferred_element_type=F32).astype(BF)
    blocks[...] = turned.reshape(4, total // 4, width)
    for f in range(4):
        outs[f][...] = blocks[me ^ f]


def turn_out(pos, array, *after):
    width, total = array.shape
    return pl.pallas_call(
        turn_out_kernel,
        in_specs=[SMEM, VMEM] + [ANY] * len(after),
        out_specs=[VMEM] * 4,
        out_shape=[jax.ShapeDtypeStruct((total // 4, width), BF)] * 4,
        scratch_shapes=[pltpu.VMEM((4, total // 4, width), BF)],
        compiler_params=SMALL,
        name="turn_out",
    )(pos, array, *after)


def exchange_slot(pos_ref, block, fy):
    x, l = pos_ref[3], pos_ref[4]
    d = ((block // NL - x) * sign(x, fy)) & (NX - 1)
    return d ^ (d >> 1), (block % NL) ^ l


def key_lanes(block, rows):
    y, z = block // NX, 2 * (block % NX)
    return [slice(((z + u) * 2 + y) * 2 * rows, ((z + u) * 2 + y + 1) * 2 * rows) for u in (0, 1)]


def bias_kernel(rows, keys, pos_ref, reach_ref, chain_ref, near_ref, far_ref, _, out_ref):
    for block in range(NX * NL):
        hot = (chain_ref[:, block * keys : (block + 1) * keys] == iota((8, keys), 0)).astype(BF)
        reach = jnp.dot(reach_ref[...], hot, preferred_element_type=F32)
        lanes = key_lanes(block, rows)
        for fy in range(NY):
            n, fl = exchange_slot(pos_ref, block, fy)
            for fc, ref in enumerate((near_ref, far_ref)):
                at = slice((2 * fy + fc) * rows, (2 * fy + fc + 1) * rows)
                value = jnp.where(reach[at] > 0.5, ref[fy, n, fl].astype(F32) * LOG2E, MASKED)
                out_ref[at, lanes[0]] = value[:, : 2 * rows]
                out_ref[at, lanes[1]] = value[:, 2 * rows :]


def attn_kernel(rows, keys, pos_ref, *refs):
    tokens = 32 * rows
    R = 4 * rows
    cols = HALF
    w = cols * DH
    qgo_refs, kv_ref, b2_ref = refs[:4], refs[4], refs[5]
    dq_out, (dkv_out, own_out, other_out), refs = refs[6:10], refs[10:13], refs[13:]
    kvt, b2, qcat, gcat, qt, gt, t_ref, acc, sums, dq_acc, db_ref, own, other = refs[:13]
    in_sem, b2_sem, out_sem, db_sem = refs[13:]
    ins = [
        pltpu.make_async_copy(kv_ref.at[n], kvt.at[:, pl.ds(n * R, R)], in_sem.at[n])
        for n in range(NZ)
    ]
    ins.append(pltpu.make_async_copy(b2_ref, b2, b2_sem))
    for copy in ins:
        copy.start()
    eye_w = (iota((w, w), 0) == iota((w, w), 1)).astype(BF)
    q, g, o = (
        jnp.concatenate(
            [qgo_refs[f][:, u * w : (u + 1) * w] for f in range(4)], axis=0
        )
        for u in range(3)
    )
    qt[...] = lax.dot_general(eye_w, q, NT, preferred_element_type=F32).astype(BF)
    gt[...] = lax.dot_general(eye_w, g, NT, preferred_element_type=F32).astype(BF)
    qs = q.astype(F32) * (SCALE * LOG2E)
    q_hi = qs.astype(BF)
    q_lo = (qs - q_hi.astype(F32)).astype(BF)
    go = g.astype(F32) * o.astype(F32)
    go_hi = go.astype(BF)
    go_lo = (go - go_hi.astype(F32)).astype(BF)
    for c in range(cols):
        d = slice(c * DH, (c + 1) * DH)
        qcat[c] = jnp.concatenate([q_hi[:, d], q_lo[:, d]], axis=1)
        gcat[c] = jnp.concatenate([g[:, d], go_hi[:, d], go_lo[:, d]], axis=1)
    db_ref[...] = jnp.zeros_like(db_ref)
    for copy in ins:
        copy.wait()
    minus = jnp.full((2 * DH, PART), -1.0, BF)
    per_column = R // BLOCK
    blocks = cols * per_column
    parts = [slice(u, u + PART) for u in range(0, tokens, PART)]

    def fold(combine, running, array):
        for u in range(0, PART, 128):
            running = combine(running, array[:, u : u + 128])
        return running

    def places(i):
        c, r = i // per_column, i % per_column
        return (
            c,
            pl.ds(pl.multiple_of(c * DH, DH), DH),
            pl.ds(pl.multiple_of(w + c * DH, DH), DH),
            pl.ds(pl.multiple_of(r * BLOCK, BLOCK), BLOCK),
            r,
        )

    def score(i, slot, part, top):
        c, k_at, _, at, _ = places(i)
        k = kvt[k_at, part]
        t = jnp.dot(qcat[c, at, :], jnp.concatenate([k, k], axis=0), preferred_element_type=F32)
        t = t + b2[at, part]
        t_ref[slot, :, part] = t
        return fold(jnp.maximum, top, t)

    def power(slot, part, top, total):
        p = jnp.exp2(t_ref[slot, :, part] - top)
        t_ref[slot, :, part] = p
        return fold(jnp.add, total, p)

    def grads(i, part, inverse, dq):
        c, k_at, v_at, at, r = places(i)
        v = jnp.concatenate([kvt[v_at, part], minus], axis=0)
        dp = jnp.dot(gcat[c, at, :], v, preferred_element_type=F32)
        weights = t_ref[i % 3, :, part] * inverse
        dl = weights * dp
        db_ref[at, part] += dl
        w_half, dl_half = weights.astype(BF), dl.astype(BF)
        dk = jnp.dot(qt[k_at, at], dl_half, preferred_element_type=F32)
        dv = jnp.dot(gt[k_at, at], w_half, preferred_element_type=F32)
        dk = jnp.where(r == 0, 0.0, sums[0, :, part]) + dk
        dv = jnp.where(r == 0, 0.0, sums[1, :, part]) + dv
        sums[0, :, part] = dk
        sums[1, :, part] = dv
        acc[k_at, part] = (dk * SCALE).astype(BF)
        acc[v_at, part] = dv.astype(BF)
        return dq + lax.dot_general(dl_half, kvt[k_at, part], NT, preferred_element_type=F32)

    lowest = jnp.full((BLOCK, 128), -3.0e38, F32)
    zero = jnp.zeros((BLOCK, 128), F32)

    def highest(top):
        return jnp.max(top, axis=1, keepdims=True)

    def inverted(total):
        return 1.0 / jnp.sum(total, axis=1, keepdims=True)

    top0, top1, total0 = lowest, lowest, zero
    for part in parts:
        top0 = score(0, 0, part, top0)
    top0 = highest(top0)
    for part in parts:
        total0 = power(0, part, top0, total0)
        top1 = score(1, 1, part, top1)

    def step(i, carry):
        top, inverse = carry
        later = jnp.minimum(i + 2, blocks - 1)
        new_top, total, dq = lowest, zero, jnp.zeros((BLOCK, DH), F32)
        for part in parts:
            dq = grads(i, part, inverse, dq)
            total = power((i + 1) % 3, part, top, total)
            new_top = score(later, (i + 2) % 3, part, new_top)
        c, _, _, at, _ = places(i)
        dq_acc[c, at, :] = dq
        return highest(new_top), inverted(total)

    lax.fori_loop(0, blocks, step, (highest(top1), inverted(total0)))
    for f in range(4):
        at = slice(f * rows, (f + 1) * rows)
        dq = jnp.concatenate([dq_acc[c, at, :] for c in range(cols)], axis=1)
        dq_out[f][...] = (dq * SCALE).astype(BF)
    outs = [
        pltpu.make_async_copy(acc.at[:, pl.ds(n * R, R)], dkv_out.at[n], out_sem.at[n])
        for n in range(NZ)
    ]
    for copy in outs:
        copy.start()
    for fc, (stage, out) in enumerate(((own, own_out), (other, other_out))):
        for fy in range(NY):
            for block in range(NX * NL):
                lanes = key_lanes(block, rows)
                n, fl = exchange_slot(pos_ref, block, fy)
                at = slice((2 * fy + fc) * rows, (2 * fy + fc + 1) * rows)
                part = jnp.concatenate([db_ref[at, lanes[0]], db_ref[at, lanes[1]]], axis=1)
                stage[fy, n, fl] = part.astype(stage.dtype)
            copy = pltpu.make_async_copy(stage.at[fy], out.at[fy], db_sem.at[2 * fc + fy])
            copy.start()
            outs.append(copy)
    for copy in outs:
        copy.wait()


def attn(pos, rows, keys, qgo, kv, b2):
    cols = HALF
    R, tokens, w = 4 * rows, 32 * rows, cols * DH
    outs = [
        *[jax.ShapeDtypeStruct((rows, w), BF)] * 4,
        jax.ShapeDtypeStruct((NZ, 2 * w, R), BF),
        jax.ShapeDtypeStruct((NY, NX, NL, rows, keys), F32),
        jax.ShapeDtypeStruct((NY, NX, NL, rows, keys), BF),
    ]
    scratch = [
        pltpu.VMEM((2 * w, tokens), BF),
        pltpu.VMEM((R, tokens), F32),
        pltpu.VMEM((cols, R, 2 * DH), BF),
        pltpu.VMEM((cols, R, 3 * DH), BF),
        pltpu.VMEM((w, R), BF),
        pltpu.VMEM((w, R), BF),
        pltpu.VMEM((3, BLOCK, tokens), F32),
        pltpu.VMEM((2 * w, tokens), BF),
        pltpu.VMEM((2, DH, tokens), F32),
        pltpu.VMEM((cols, R, DH), F32),
        pltpu.VMEM((R, tokens), F32),
        pltpu.VMEM((NY, NX, NL, rows, keys), F32),
        pltpu.VMEM((NY, NX, NL, rows, keys), BF),
        pltpu.SemaphoreType.DMA((NZ,)),
        pltpu.SemaphoreType.DMA,
        pltpu.SemaphoreType.DMA((NZ,)),
        pltpu.SemaphoreType.DMA((2 * NY,)),
    ]
    ins = [*qgo, kv, b2]
    return pl.pallas_call(
        functools.partial(attn_kernel, rows, keys),
        in_specs=[SMEM] + [VMEM] * 4 + [HBM, ANY],
        out_specs=[VMEM] * 4 + [HBM] * 3,
        out_shape=outs,
        scratch_shapes=scratch,
        compiler_params=LARGE,
        cost_estimate=pl.CostEstimate(
            flops=9 * 10**9 * cols, bytes_accessed=10 * R * tokens, transcendentals=R * tokens * cols
        ),
        name="attn",
    )(pos, *ins)


def per_device(
    queries, key_rows, value_rows, saved_output, grad_output, pair_bias, chain_id, allowed_pairs
):
    rows, width = queries.shape
    keys = pair_bias.shape[2]
    row_index = lax.axis_index("row")
    col_index = lax.axis_index("col")
    y, z, c = row_index // (NZ * NC), (row_index // NC) % NZ, row_index % NC
    me = y * 2 + c
    pos = jnp.stack([me, y, z, col_index // NL, col_index % NL]).astype(jnp.int32)

    groups = [
        [(y * NZ + z) * NC + c for z in range(NZ)] for y in range(NY) for c in range(NC)
    ]
    bias_own = lax.dynamic_index_in_dim(pair_bias, y, 0, keepdims=False)
    bias_other = lax.dynamic_index_in_dim(pair_bias, 1 - y, 0, keepdims=False)
    bias_rows = (bias_own, row_move(bias_other, 1, 0, 0))

    kv_far = split((2, 3), (key_rows, value_rows))
    kv_near = split((0, 1), (key_rows, value_rows), kv_far[0])
    kv_parts = swap([*kv_near, *kv_far])
    kv = lax.all_gather(turn_in(pos, kv_parts), "row", axis_index_groups=groups)
    rest = swap(split((0, 1, 2, 3), (queries, grad_output, saved_output), kv_parts[3]))

    labels = jnp.arange(allowed_pairs.shape[0], dtype=jnp.int32)
    chains = chain_id.reshape(NY, NZ, NC, rows)
    chains = lax.dynamic_index_in_dim(chains, z, 1, keepdims=False)
    chains = jnp.stack(
        [
            lax.dynamic_slice(chains, (y ^ fy, c ^ fc, 0), (1, 1, rows)).reshape(rows)
            for fy, fc in ((0, 0), (0, 1), (1, 0), (1, 1))
        ]
    ).reshape(4 * rows)
    reach = jnp.dot(
        (chains[:, None] == labels[None, :]).astype(F32), (allowed_pairs == 1).astype(F32)
    ).astype(BF)
    bias_lanes = col_move(jnp.stack(bias_rows), 0, 1)
    bias_near = []
    for fy in range(NY):
        own = jnp.stack([bias_rows[fy], bias_lanes[fy]])
        both = jnp.stack([own, x_pair(own, fy, 1)])
        bias_near += [both, x_pair(both, fy, -1)]
    bias_near = jnp.stack([jnp.concatenate(bias_near[:2]), jnp.concatenate(bias_near[2:])])
    bias_far = row_move(bias_near, 0, 0, 1)
    b2 = pl.pallas_call(
        functools.partial(bias_kernel, rows, keys),
        in_specs=[SMEM] + [VMEM] * 4 + [HBM],
        out_specs=VMEM,
        out_shape=jax.ShapeDtypeStruct((4 * rows, 32 * rows), F32),
        compiler_params=SMALL,
        name="bias",
    )(pos, reach, chain_id.reshape(1, -1), bias_near, bias_far, kv)

    *dq, dkv, db_own, db_other = attn(pos, rows, keys, rest, kv, b2)
    summed = lax.psum_scatter(
        dkv.reshape(NZ * 2 * HALF * DH, 4 * rows),
        "row",
        scatter_dimension=0,
        axis_index_groups=groups,
        tiled=True,
    )
    (grad_q,) = join(pos, width, swap(dq), 1)

    db_sum = (db_own + row_move(db_other, 0, 0, 1).astype(F32)).astype(BF)
    total = []
    for fy in range(NY):
        part = x_pair(db_sum[fy, 2:], fy, -1).astype(F32) + db_sum[fy, :2].astype(F32)
        total.append(part[0] + x_pair(part[1].astype(BF), fy, 1).astype(F32))
    total = jnp.stack(total)
    total = total[:, 0] + col_move(total[:, 1].astype(BF), 0, 1).astype(F32)
    total = total.astype(BF)
    got = row_move(total[1], 1, 0, 0)
    grad_bias = jnp.where(
        y == 0, jnp.stack([total[0], got]), jnp.stack([got, total[0]])
    )
    back = swap(turn_out(pos, summed, grad_q, grad_bias))
    grad_k, grad_v = join(pos, width, back, 2)
    return grad_q, grad_k, grad_v, grad_bias


def solution(mesh):
    whole = P("row", "col")
    bias = P(None, "row", "col")
    return jax.shard_map(
        per_device,
        mesh=mesh,
        in_specs=(whole,) * 5 + (bias, P(), P()),
        out_specs=(whole, whole, whole, bias),
        check_vma=False,
    )
```

```python
import functools
import math

import jax
import jax.numpy as jnp
from jax import lax
from jax.experimental import pallas as pl
from jax.experimental.pallas import tpu as pltpu
from jax.sharding import PartitionSpec as P

H = 2
DH = 32
SCALE = 1.0 / math.sqrt(DH)
LOG2E = math.log2(math.e)
MASKED = -1000000000.0 * LOG2E
NY, NZ, NC = 2, 8, 2
NX, NL = 4, 2
HALF = 7
BLOCK = 128
PART = 3072

F32 = jnp.float32
BF = jnp.bfloat16
NT = (((1,), (1,)), ((), ()))
VMEM = pl.BlockSpec(memory_space=pltpu.VMEM)
SMEM = pl.BlockSpec(memory_space=pltpu.SMEM)
ANY = pl.BlockSpec(memory_space=pl.ANY)
HBM = pl.BlockSpec(memory_space=pltpu.HBM)
SMALL = pltpu.CompilerParams(vmem_limit_bytes=16 * 2**20)
LARGE = pltpu.CompilerParams(vmem_limit_bytes=34 * 2**20)


def iota(shape, dim):
    return lax.broadcasted_iota(jnp.int32, shape, dim)


def row_move(array, dy, dz, dc):
    pairs = []
    for y in range(NY):
        for z in range(NZ):
            for c in range(NC):
                target = ((y ^ dy) * NZ + (z + dz) % NZ) * NC + (c ^ dc)
                pairs.append(((y * NZ + z) * NC + c, target))
    return lax.ppermute(array, "row", pairs)


def col_move(array, dx, dl):
    pairs = []
    for x in range(NX):
        for l in range(NL):
            pairs.append((x * NL + l, ((x + dx) % NX) * NL + (l ^ dl)))
    return lax.ppermute(array, "col", pairs)


def sign(index, half):
    even = 1 - 2 * (index % 2)
    return even if half == 0 else -even


def x_pair(array, half, way):
    pairs = []
    for x in range(NX):
        for l in range(NL):
            pairs.append((x * NL + l, ((x + way * sign(x, half)) % NX) * NL + l))
    return lax.ppermute(array, "col", pairs)


def picks(shape, dim):
    mine = iota(shape, dim)
    distance = iota(shape, 1 - dim) - 2 * mine + (mine & (DH - 1))

    def pick(owner):
        return (distance == (owner % 2) * (HALF * H * DH) + (owner // 2) * DH).astype(BF)

    return pick


def split_kernel(count, flips, *refs):
    ins, outs = refs[:count], refs[-len(flips) :]
    row = lax.axis_index("row")
    me = (row // (NZ * NC)) * 2 + row % NC
    width = ins[0].shape[1]
    w = HALF * DH
    pick = picks((width, w), 1)
    for out, f in zip(outs, flips):
        chosen = pick(me ^ f)
        for u in range(count):
            out[:, u * w : (u + 1) * w] = jnp.dot(
                ins[u][...], chosen, preferred_element_type=F32
            ).astype(BF)


def split(flips, arrays, *after):
    rows = arrays[0].shape[0]
    return pl.pallas_call(
        functools.partial(split_kernel, len(arrays), flips),
        in_specs=[VMEM] * len(arrays) + [ANY] * len(after),
        out_specs=[VMEM] * len(flips),
        out_shape=[jax.ShapeDtypeStruct((rows, len(arrays) * HALF * DH), BF)] * len(flips),
        compiler_params=SMALL,
        name="split",
    )(*arrays, *after)


def swap(parts):
    return [
        part if f == 0 else row_move(part, f // 2, 0, f % 2) for f, part in enumerate(parts)
    ]


def join_kernel(count, me_ref, *refs):
    parts, outs = refs[:4], refs[-count:]
    rows, width = outs[0].shape
    w = HALF * DH
    pick = picks((w, width), 0)
    sums = [jnp.zeros((rows, width), F32)] * count
    for f in range(4):
        chosen = pick(me_ref[0] ^ f)
        for u in range(count):
            sums[u] = sums[u] + jnp.dot(
                parts[f][:, u * w : (u + 1) * w], chosen, preferred_element_type=F32
            )
    for u in range(count):
        outs[u][...] = sums[u].astype(BF)


def join(pos, width, parts, count):
    rows = parts[0].shape[0]
    return pl.pallas_call(
        functools.partial(join_kernel, count),
        in_specs=[SMEM] + [VMEM] * 4,
        out_specs=[VMEM] * count,
        out_shape=[jax.ShapeDtypeStruct((rows, width), BF)] * count,
        compiler_params=SMALL,
        name="join",
    )(pos, *parts)


def turn_in_kernel(pos_ref, *refs):
    parts, out = refs[:4], refs[-1]
    me = pos_ref[0]
    rows, width = parts[0].shape
    blocks = refs[-2]
    for f in range(4):
        blocks[me ^ f] = parts[f][...]
    del refs
    eye = (iota((width, width), 0) == iota((width, width), 1)).astype(BF)
    out[...] = lax.dot_general(
        eye, blocks[...].reshape(4 * rows, width), NT, preferred_element_type=F32
    ).astype(BF)


def turn_in(pos, parts):
    rows, width = parts[0].shape
    return pl.pallas_call(
        lambda pos_ref, *refs: turn_in_kernel(pos_ref, *refs[:4], refs[5], refs[4]),
        in_specs=[SMEM] + [VMEM] * 4,
        out_specs=VMEM,
        out_shape=jax.ShapeDtypeStruct((width, 4 * rows), BF),
        scratch_shapes=[pltpu.VMEM((4, rows, width), BF)],
        compiler_params=SMALL,
        name="turn_in",
    )(pos, *parts)


def turn_out_kernel(pos_ref, in_ref, *refs):
    outs, blocks = refs[-5:-1], refs[-1]
    me = pos_ref[0]
    width, total = in_ref.shape
    eye = (iota((total, total), 0) == iota((total, total), 1)).astype(BF)
    turned = lax.dot_general(eye, in_ref[...], NT, preferred_element_type=F32).astype(BF)
    blocks[...] = turned.reshape(4, total // 4, width)
    for f in range(4):
        outs[f][...] = blocks[me ^ f]


def turn_out(pos, array, *after):
    width, total = array.shape
    return pl.pallas_call(
        turn_out_kernel,
        in_specs=[SMEM, VMEM] + [ANY] * len(after),
        out_specs=[VMEM] * 4,
        out_shape=[jax.ShapeDtypeStruct((total // 4, width), BF)] * 4,
        scratch_shapes=[pltpu.VMEM((4, total // 4, width), BF)],
        compiler_params=SMALL,
        name="turn_out",
    )(pos, array, *after)


def exchange_slot(pos_ref, block, fy):
    x, l = pos_ref[3], pos_ref[4]
    d = ((block // NL - x) * sign(x, fy)) & (NX - 1)
    return d ^ (d >> 1), (block % NL) ^ l


def key_lanes(block, rows):
    y, z = block // NX, 2 * (block % NX)
    return [slice(((z + u) * 2 + y) * 2 * rows, ((z + u) * 2 + y + 1) * 2 * rows) for u in (0, 1)]


def bias_kernel(rows, keys, pos_ref, reach_ref, chain_ref, near_ref, far_ref, _, out_ref):
    for block in range(NX * NL):
        hot = (chain_ref[:, block * keys : (block + 1) * keys] == iota((8, keys), 0)).astype(BF)
        reach = jnp.dot(reach_ref[...], hot, preferred_element_type=F32)
        lanes = key_lanes(block, rows)
        for fy in range(NY):
            n, fl = exchange_slot(pos_ref, block, fy)
            for fc, ref in enumerate((near_ref, far_ref)):
                at = slice((2 * fy + fc) * rows, (2 * fy + fc + 1) * rows)
                value = jnp.where(reach[at] > 0.5, ref[fy, n, fl].astype(F32) * LOG2E, MASKED)
                out_ref[at, lanes[0]] = value[:, : 2 * rows]
                out_ref[at, lanes[1]] = value[:, 2 * rows :]


def attn_kernel(rows, keys, pos_ref, *refs):
    tokens = 32 * rows
    R = 4 * rows
    cols = HALF
    w = cols * DH
    qgo_refs, kv_ref, b2_ref = refs[:4], refs[4], refs[5]
    dq_out, (dkv_out, own_out, other_out), refs = refs[6:10], refs[10:13], refs[13:]
    kvt, b2, qcat, gcat, qt, gt, t_ref, acc, sums, dq_acc, db_ref, own, other = refs[:13]
    in_sem, b2_sem, out_sem, db_sem = refs[13:]
    ins = [
        pltpu.make_async_copy(kv_ref.at[n], kvt.at[:, pl.ds(n * R, R)], in_sem.at[n])
        for n in range(NZ)
    ]
    ins.append(pltpu.make_async_copy(b2_ref, b2, b2_sem))
    for copy in ins:
        copy.start()
    eye_w = (iota((w, w), 0) == iota((w, w), 1)).astype(BF)
    q, g, o = (
        jnp.concatenate(
            [qgo_refs[f][:, u * w : (u + 1) * w] for f in range(4)], axis=0
        )
        for u in range(3)
    )
    qt[...] = lax.dot_general(eye_w, q, NT, preferred_element_type=F32).astype(BF)
    gt[...] = lax.dot_general(eye_w, g, NT, preferred_element_type=F32).astype(BF)
    qs = q.astype(F32) * (SCALE * LOG2E)
    q_hi = qs.astype(BF)
    q_lo = (qs - q_hi.astype(F32)).astype(BF)
    go = g.astype(F32) * o.astype(F32)
    go_hi = go.astype(BF)
    go_lo = (go - go_hi.astype(F32)).astype(BF)
    for c in range(cols):
        d = slice(c * DH, (c + 1) * DH)
        qcat[c] = jnp.concatenate([q_hi[:, d], q_lo[:, d]], axis=1)
        gcat[c] = jnp.concatenate([g[:, d], go_hi[:, d], go_lo[:, d]], axis=1)
    db_ref[...] = jnp.zeros_like(db_ref)
    for copy in ins:
        copy.wait()
    minus = jnp.full((2 * DH, PART), -1.0, BF)
    per_column = R // BLOCK
    blocks = cols * per_column
    parts = [slice(u, u + PART) for u in range(0, tokens, PART)]

    def fold(combine, running, array):
        for u in range(0, PART, 128):
            running = combine(running, array[:, u : u + 128])
        return running

    def places(i):
        c, r = i // per_column, i % per_column
        return (
            c,
            pl.ds(pl.multiple_of(c * DH, DH), DH),
            pl.ds(pl.multiple_of(w + c * DH, DH), DH),
            pl.ds(pl.multiple_of(r * BLOCK, BLOCK), BLOCK),
            r,
        )

    def score(i, slot, part, top):
        c, k_at, _, at, _ = places(i)
        k = kvt[k_at, part]
        t = jnp.dot(qcat[c, at, :], jnp.concatenate([k, k], axis=0), preferred_element_type=F32)
        t = t + b2[at, part]
        t_ref[slot, :, part] = t
        return fold(jnp.maximum, top, t)

    def power(slot, part, top, total):
        p = jnp.exp2(t_ref[slot, :, part] - top)
        t_ref[slot, :, part] = p
        return fold(jnp.add, total, p)

    def grads(i, part, inverse, dq):
        c, k_at, v_at, at, r = places(i)
        v = jnp.concatenate([kvt[v_at, part], minus], axis=0)
        dp = jnp.dot(gcat[c, at, :], v, preferred_element_type=F32)
        weights = t_ref[i % 3, :, part] * inverse
        dl = weights * dp
        db_ref[at, part] += dl
        w_half, dl_half = weights.astype(BF), dl.astype(BF)
        dk = jnp.dot(qt[k_at, at], dl_half, preferred_element_type=F32)
        dv = jnp.dot(gt[k_at, at], w_half, preferred_element_type=F32)
        dk = jnp.where(r == 0, 0.0, sums[0, :, part]) + dk
        dv = jnp.where(r == 0, 0.0, sums[1, :, part]) + dv
        sums[0, :, part] = dk
        sums[1, :, part] = dv
        acc[k_at, part] = (dk * SCALE).astype(BF)
        acc[v_at, part] = dv.astype(BF)
        return dq + lax.dot_general(dl_half, kvt[k_at, part], NT, preferred_element_type=F32)

    lowest = jnp.full((BLOCK, 128), -3.0e38, F32)
    zero = jnp.zeros((BLOCK, 128), F32)

    def highest(top):
        return jnp.max(top, axis=1, keepdims=True)

    def inverted(total):
        return 1.0 / jnp.sum(total, axis=1, keepdims=True)

    top0, top1, total0 = lowest, lowest, zero
    for part in parts:
        top0 = score(0, 0, part, top0)
    top0 = highest(top0)
    for part in parts:
        total0 = power(0, part, top0, total0)
        top1 = score(1, 1, part, top1)

    def step(i, carry):
        top, inverse = carry
        later = jnp.minimum(i + 2, blocks - 1)
        new_top, total, dq = lowest, zero, jnp.zeros((BLOCK, DH), F32)
        for part in parts:
            dq = grads(i, part, inverse, dq)
            total = power((i + 1) % 3, part, top, total)
            new_top = score(later, (i + 2) % 3, part, new_top)
        c, _, _, at, _ = places(i)
        dq_acc[c, at, :] = dq
        return highest(new_top), inverted(total)

    lax.fori_loop(0, blocks, step, (highest(top1), inverted(total0)))
    for f in range(4):
        at = slice(f * rows, (f + 1) * rows)
        dq = jnp.concatenate([dq_acc[c, at, :] for c in range(cols)], axis=1)
        dq_out[f][...] = (dq * SCALE).astype(BF)
    outs = [
        pltpu.make_async_copy(acc.at[:, pl.ds(n * R, R)], dkv_out.at[n], out_sem.at[n])
        for n in range(NZ)
    ]
    for copy in outs:
        copy.start()
    for fc, (stage, out) in enumerate(((own, own_out), (other, other_out))):
        for fy in range(NY):
            for block in range(NX * NL):
                lanes = key_lanes(block, rows)
                n, fl = exchange_slot(pos_ref, block, fy)
                at = slice((2 * fy + fc) * rows, (2 * fy + fc + 1) * rows)
                part = jnp.concatenate([db_ref[at, lanes[0]], db_ref[at, lanes[1]]], axis=1)
                stage[fy, n, fl] = part.astype(stage.dtype)
            copy = pltpu.make_async_copy(stage.at[fy], out.at[fy], db_sem.at[2 * fc + fy])
            copy.start()
            outs.append(copy)
    for copy in outs:
        copy.wait()


def attn(pos, rows, keys, qgo, kv, b2):
    cols = HALF
    R, tokens, w = 4 * rows, 32 * rows, cols * DH
    outs = [
        *[jax.ShapeDtypeStruct((rows, w), BF)] * 4,
        jax.ShapeDtypeStruct((NZ, 2 * w, R), BF),
        jax.ShapeDtypeStruct((NY, NX, NL, rows, keys), F32),
        jax.ShapeDtypeStruct((NY, NX, NL, rows, keys), BF),
    ]
    scratch = [
        pltpu.VMEM((2 * w, tokens), BF),
        pltpu.VMEM((R, tokens), F32),
        pltpu.VMEM((cols, R, 2 * DH), BF),
        pltpu.VMEM((cols, R, 3 * DH), BF),
        pltpu.VMEM((w, R), BF),
        pltpu.VMEM((w, R), BF),
        pltpu.VMEM((3, BLOCK, tokens), F32),
        pltpu.VMEM((2 * w, tokens), BF),
        pltpu.VMEM((2, DH, tokens), F32),
        pltpu.VMEM((cols, R, DH), F32),
        pltpu.VMEM((R, tokens), F32),
        pltpu.VMEM((NY, NX, NL, rows, keys), F32),
        pltpu.VMEM((NY, NX, NL, rows, keys), BF),
        pltpu.SemaphoreType.DMA((NZ,)),
        pltpu.SemaphoreType.DMA,
        pltpu.SemaphoreType.DMA((NZ,)),
        pltpu.SemaphoreType.DMA((2 * NY,)),
    ]
    ins = [*qgo, kv, b2]
    return pl.pallas_call(
        functools.partial(attn_kernel, rows, keys),
        in_specs=[SMEM] + [VMEM] * 4 + [HBM, ANY],
        out_specs=[VMEM] * 4 + [HBM] * 3,
        out_shape=outs,
        scratch_shapes=scratch,
        compiler_params=LARGE,
        cost_estimate=pl.CostEstimate(
            flops=9 * 10**9 * cols, bytes_accessed=10 * R * tokens, transcendentals=R * tokens * cols
        ),
        name="attn",
    )(pos, *ins)


def per_device(
    queries, key_rows, value_rows, saved_output, grad_output, pair_bias, chain_id, allowed_pairs
):
    rows, width = queries.shape
    keys = pair_bias.shape[2]
    row_index = lax.axis_index("row")
    col_index = lax.axis_index("col")
    y, z, c = row_index // (NZ * NC), (row_index // NC) % NZ, row_index % NC
    me = y * 2 + c
    pos = jnp.stack([me, y, z, col_index // NL, col_index % NL]).astype(jnp.int32)

    groups = [
        [(y * NZ + z) * NC + c for z in range(NZ)] for y in range(NY) for c in range(NC)
    ]
    bias_own = lax.dynamic_index_in_dim(pair_bias, y, 0, keepdims=False)
    bias_other = lax.dynamic_index_in_dim(pair_bias, 1 - y, 0, keepdims=False)
    bias_rows = (bias_own, row_move(bias_other, 1, 0, 0))

    kv_far = split((2, 3), (key_rows, value_rows))
    kv_near = split((0, 1), (key_rows, value_rows), kv_far[0])
    kv_parts = swap([*kv_near, *kv_far])
    kv = lax.all_gather(turn_in(pos, kv_parts), "row", axis_index_groups=groups)
    rest = swap(split((0, 1, 2, 3), (queries, grad_output, saved_output), kv_parts[3]))

    labels = jnp.arange(allowed_pairs.shape[0], dtype=jnp.int32)
    chains = chain_id.reshape(NY, NZ, NC, rows)
    chains = lax.dynamic_index_in_dim(chains, z, 1, keepdims=False)
    chains = jnp.stack(
        [
            lax.dynamic_slice(chains, (y ^ fy, c ^ fc, 0), (1, 1, rows)).reshape(rows)
            for fy, fc in ((0, 0), (0, 1), (1, 0), (1, 1))
        ]
    ).reshape(4 * rows)
    reach = jnp.dot(
        (chains[:, None] == labels[None, :]).astype(F32), (allowed_pairs == 1).astype(F32)
    ).astype(BF)
    bias_lanes = col_move(jnp.stack(bias_rows), 0, 1)
    bias_near = []
    for fy in range(NY):
        own = jnp.stack([bias_rows[fy], bias_lanes[fy]])
        both = jnp.stack([own, x_pair(own, fy, 1)])
        bias_near += [both, x_pair(both, fy, -1)]
    bias_near = jnp.stack([jnp.concatenate(bias_near[:2]), jnp.concatenate(bias_near[2:])])
    bias_far = row_move(bias_near, 0, 0, 1)
    b2 = pl.pallas_call(
        functools.partial(bias_kernel, rows, keys),
        in_specs=[SMEM] + [VMEM] * 4 + [ANY],
        out_specs=VMEM,
        out_shape=jax.ShapeDtypeStruct((4 * rows, 32 * rows), F32),
        compiler_params=SMALL,
        name="bias",
    )(pos, reach, chain_id.reshape(1, -1), bias_near, bias_far, kv[0, :16, :128])

    *dq, dkv, db_own, db_other = attn(pos, rows, keys, rest, kv, b2)
    summed = lax.psum_scatter(
        dkv.reshape(NZ * 2 * HALF * DH, 4 * rows),
        "row",
        scatter_dimension=0,
        axis_index_groups=groups,
        tiled=True,
    )
    dq_parts = swap(dq)
    (grad_q,) = join(pos, width, dq_parts, 1)

    db_sum = (db_own + row_move(db_other, 0, 0, 1).astype(F32)).astype(BF)
    total = []
    for fy in range(NY):
        part = x_pair(db_sum[fy, 2:], fy, -1).astype(F32) + db_sum[fy, :2].astype(F32)
        total.append(part[0] + x_pair(part[1].astype(BF), fy, 1).astype(F32))
    total = jnp.stack(total)
    total = total[:, 0] + col_move(total[:, 1].astype(BF), 0, 1).astype(F32)
    total = total.astype(BF)
    got = row_move(total[1], 1, 0, 0)
    grad_bias = jnp.where(
        y == 0, jnp.stack([total[0], got]), jnp.stack([got, total[0]])
    )
    back = swap(turn_out(pos, summed, *dq_parts[1:], grad_bias))
    grad_k, grad_v = join(pos, width, back, 2)
    return grad_q, grad_k, grad_v, grad_bias


def solution(mesh):
    whole = P("row", "col")
    bias = P(None, "row", "col")
    return jax.shard_map(
        per_device,
        mesh=mesh,
        in_specs=(whole,) * 5 + (bias, P(), P()),
        out_specs=(whole, whole, whole, bias),
        check_vma=False,
    )
```
